256 devices in a mesh: lon: 16 (over y, x_hi, core), lat: 16 (over z, x_lo).
Axes of the slice: x: 4 (x_hi: 2, x_lo: 2; x = x_hi * 2 + x_lo), y: 4, z: 8, core: 2. Of those that a mesh axis runs over, the one named last changes fastest.
Arguments:
- potential_warmth: float32 [75, 128, 2048], P(None, 'lat', 'lon'), may hold values from -6 to 6
- saltiness_anomaly: float32 [75, 128, 2048], P(None, 'lat', 'lon'), may hold values from -6 to 6
- zonal_current: float32 [75, 128, 2048], P(None, 'lat', 'lon'), may hold values from -3 to 3
- meridional_current: float32 [75, 128, 2048], P(None, 'lat', 'lon'), may hold values from -3 to 3
- marine_indicator: int32 [75, 128, 2048], P(None, 'lat', 'lon'), may hold values 0 or 1
- bathymetry_layers: int32 [128, 2048], P('lat', 'lon'), may hold values from 1 to 75
- planetary_vorticity: float32 [128, 2048], P('lat', 'lon'), may hold values from -1.5 to 1.5
Outputs:
- temp_next: float32 [75, 128, 2048], P(None, 'lat', 'lon')
- salt_next: float32 [75, 128, 2048], P(None, 'lat', 'lon')
- east_next: float32 [75, 128, 2048], P(None, 'lat', 'lon')
- north_next: float32 [75, 128, 2048], P(None, 'lat', 'lon')
The draws below stay inside these ranges and needn't reach their ends.
All inputs are finite; a program needn't handle non-finite values. No bound on the sum of `marine_indicator` on one device may be relied on, other than what follows from the above.
Results may differ from the reference program's by a relative error of at most 0.0003.
Values sent between devices are 32-bit elements; how exact they have to be, the bound alone decides.
No kernel may reach another device: no remote copies, remote signals or barrier semaphores. Data moves between devices by JAX's collectives and lax.ppermute only.
A program may use at most 128 MiB of HBM per device.

```python
import jax
import jax.numpy as jnp
from jax import lax

DEPTH_LAYERS = 75
ITERS = 2
PARALLEL_POINTS = 2048
MERIDIAN_POINTS = 128
N_LAT = 16


def still_cells(key):
    extent = (DEPTH_LAYERS, MERIDIAN_POINTS, PARALLEL_POINTS)
    return jax.random.randint(key, extent, 0, 10) == 0


def normal_field(key, spread, limit):
    extent = (DEPTH_LAYERS, MERIDIAN_POINTS, PARALLEL_POINTS)
    values = spread * jax.random.normal(key, extent, jnp.float32)
    return jnp.clip(values, -limit, limit)


def draw_potential_warmth(key, part):
    marks = still_cells(key)
    key = jax.random.fold_in(key, 11)
    values = normal_field(key, 1.0, 6.0)
    return jnp.where(marks, 0.0, values).astype(jnp.float32)


def draw_saltiness_anomaly(key, part):
    marks = still_cells(key)
    key = jax.random.fold_in(key, 12)
    values = normal_field(key, 1.0, 6.0)
    return jnp.where(marks, 0.0, values).astype(jnp.float32)


def draw_zonal_current(key, part):
    marks = still_cells(key)
    key = jax.random.fold_in(key, 13)
    values = normal_field(key, 0.5, 3.0)
    return jnp.where(marks, 0.0, values).astype(jnp.float32)


def draw_meridional_current(key, part):
    marks = still_cells(key)
    key = jax.random.fold_in(key, 14)
    values = normal_field(key, 0.5, 3.0)
    return jnp.where(marks, 0.0, values).astype(jnp.float32)


def draw_bathymetry_layers(key, part):
    key = jax.random.fold_in(key, 15)
    extent = (MERIDIAN_POINTS, PARALLEL_POINTS)
    pick_key, deep_key, spread_key = jax.random.split(key, 3)
    picker = jax.random.randint(pick_key, extent, 0, 5)
    deep_floor = DEPTH_LAYERS - jax.random.randint(deep_key, extent, 0, max(DEPTH_LAYERS // 8, 1))
    any_floor = jax.random.randint(spread_key, extent, 1, DEPTH_LAYERS + 1)
    floors = jnp.where(picker == 0, any_floor, deep_floor).astype(jnp.int32)
    floors = floors.at[0, 0].set(1)
    floors = floors.at[0, 1].set(DEPTH_LAYERS)
    return floors


def touch_ends(entries, own_key, low, largest):
    longest = entries.shape.index(max(entries.shape))
    spots = []
    for shift in (0, 1):
        where = [jax.random.randint(jax.random.fold_in(own_key, axis), (), 0, length) for axis, length in enumerate(entries.shape)]
        where[longest] = (where[longest] + shift) % entries.shape[longest]
        spots.append(tuple(where))
    return entries.at[spots[0]].set(low).at[spots[1]].set(largest)


def shard_levels(stream_key, shape, cuts, smallest, high):
    gain = 1.0
    for axis_at, blocks in cuts:
        draws = jax.random.uniform(jax.random.fold_in(jax.random.fold_in(stream_key, 6), axis_at), (blocks,), jnp.float32, smallest / len(cuts), high / len(cuts))
        gain = gain * jnp.repeat(jnp.exp(draws), shape[axis_at] // blocks).reshape((-1,) + (1,) * (len(shape) - 1 - axis_at))
    return gain


def setup_inputs(seed: int = 0) -> dict:
    streams_of = jax.random.split(jax.random.key(seed), 8)
    potential_warmth = draw_potential_warmth(jax.random.fold_in(streams_of[7], 71), 0)
    saltiness_anomaly = draw_saltiness_anomaly(jax.random.fold_in(streams_of[7], 71), 0)
    zonal_current = draw_zonal_current(jax.random.fold_in(streams_of[7], 71), 0)
    meridional_current = draw_meridional_current(jax.random.fold_in(streams_of[7], 71), 0)
    marine_indicator = touch_ends((jax.random.randint(streams_of[4], (DEPTH_LAYERS, MERIDIAN_POINTS, PARALLEL_POINTS), 0, 5) < 4).astype(jnp.int32), jax.random.fold_in(streams_of[4], 1), 0, 1)
    bathymetry_layers = draw_bathymetry_layers(jax.random.fold_in(streams_of[7], 71), 0)
    planetary_vorticity = jnp.clip(jax.random.uniform(streams_of[6], (MERIDIAN_POINTS, PARALLEL_POINTS), jnp.float32, -1.5, 1.5) * shard_levels(streams_of[6], (MERIDIAN_POINTS, PARALLEL_POINTS), ((0, 16), (1, 16)), -0.4, 0.0), -1.5, 1.5)
    return dict(potential_warmth=potential_warmth, saltiness_anomaly=saltiness_anomaly, zonal_current=zonal_current, meridional_current=meridional_current, marine_indicator=marine_indicator, bathymetry_layers=bathymetry_layers, planetary_vorticity=planetary_vorticity)


TIME_STEP = 0.1
SIDE_DIFF = 0.4
VERT_DIFF = 0.4
THERMAL = 0.2
HALINE = 0.8
GRAVITY = 0.1
BOTTOM_DRAG = 2.0


def advance(padded, coef_pad):
    levels = padded.shape[1]
    liquid_share = coef_pad[0, :levels]
    rotation = coef_pad[0, levels, 1:-1, 1:-1]
    floor_level = coef_pad[0, levels + 1, 1:-1, 1:-1]
    density = HALINE * padded[1] - THERMAL * padded[0]
    pressure = GRAVITY * (jnp.cumsum(density, axis=0) - 0.5 * density)
    fields = jnp.concatenate([padded, pressure[None]], axis=0)
    centre = fields[:, :, 1:-1, 1:-1]
    row_count = fields.shape[2]
    col_count = fields.shape[3]

    def beside(row_step, col_step):
        neighbour = fields[:, :, 1 + row_step:row_count - 1 + row_step, 1 + col_step:col_count - 1 + col_step]
        open_side = liquid_share[:, 1 + row_step:row_count - 1 + row_step, 1 + col_step:col_count - 1 + col_step]
        return centre + open_side * (neighbour - centre)

    east_side = beside(0, 1)
    west_side = beside(0, -1)
    north_side = beside(1, 0)
    south_side = beside(-1, 0)
    laplacian = east_side + west_side + north_side + south_side - 4.0 * centre
    slope_east = 0.5 * (east_side - west_side)
    slope_north = 0.5 * (north_side - south_side)
    interior = centre[:4]
    wet_centre = liquid_share[:, 1:-1, 1:-1]
    zero_level = jnp.zeros_like(interior[:, :1])
    upper_level = jnp.concatenate([zero_level, interior[:, :-1]], axis=1)
    lower_level = jnp.concatenate([interior[:, 1:], zero_level], axis=1)
    zero_wet = jnp.zeros_like(wet_centre[:1])
    wet_upper = jnp.concatenate([zero_wet, wet_centre[:-1]], axis=0)
    wet_lower = jnp.concatenate([wet_centre[1:], zero_wet], axis=0)
    vertical = wet_upper * (upper_level - interior) + wet_lower * (lower_level - interior)
    speed_east = interior[2]
    speed_north = interior[3]
    tendency = SIDE_DIFF * laplacian[:4] + VERT_DIFF * vertical - (speed_east * slope_east[:4] + speed_north * slope_north[:4])
    level_index = lax.broadcasted_iota(jnp.float32, wet_centre.shape, 0)
    drag_rate = jnp.where(level_index == floor_level - 1.0, BOTTOM_DRAG, 0.0)
    force_east = rotation * speed_north - slope_east[4] - drag_rate * speed_east
    force_north = -rotation * speed_east - slope_north[4] - drag_rate * speed_north
    tendency = tendency.at[2].add(force_east)
    tendency = tendency.at[3].add(force_north)
    return interior + TIME_STEP * tendency * wet_centre


def pad_global(source, fold_signs):
    widened = jnp.concatenate([source[..., -1:], source, source[..., :1]], axis=3)
    ghost_rows = jnp.flip(widened[:, :, -1:, :], axis=3) * fold_signs
    zero_rows = jnp.zeros_like(widened[:, :, :1, :])
    return jnp.concatenate([zero_rows, widened, ghost_rows], axis=2)


def reference(potential_warmth, saltiness_anomaly, zonal_current, meridional_current, marine_indicator, bathymetry_layers, planetary_vorticity):
    level_ids = lax.broadcasted_iota(jnp.int32, marine_indicator.shape, 0)
    liquid_share = jnp.where(level_ids < bathymetry_layers[None], marine_indicator, 0).astype(jnp.float32)
    coefficients = jnp.concatenate([liquid_share, planetary_vorticity[None], bathymetry_layers.astype(jnp.float32)[None]], axis=0)[None]
    plain_signs = jnp.ones((1, 1, 1, 1), jnp.float32)
    fold_signs = jnp.array([1.0, 1.0, -1.0, -1.0], jnp.float32).reshape(4, 1, 1, 1)
    coef_pad = pad_global(coefficients, plain_signs)
    current_motion_state = jnp.stack([potential_warmth, saltiness_anomaly, zonal_current, meridional_current]) * liquid_share
    band_rows = MERIDIAN_POINTS // N_LAT
    for iteration in range(ITERS):
        padded = pad_global(current_motion_state, fold_signs)

        def advance_rows(band_index):
            first_row = (band_index * band_rows).astype(jnp.int32)
            row_block = lax.dynamic_slice_in_dim(padded, first_row, band_rows + 2, axis=2)
            coef_block = lax.dynamic_slice_in_dim(coef_pad, first_row, band_rows + 2, axis=2)
            return advance(row_block, coef_block)

        bands = lax.map(advance_rows, jnp.arange(N_LAT, dtype=jnp.int32))
        current_motion_state = jnp.transpose(bands, (1, 2, 0, 3, 4)).reshape(4, DEPTH_LAYERS, MERIDIAN_POINTS, PARALLEL_POINTS)
    return current_motion_state[0], current_motion_state[1], current_motion_state[2], current_motion_state[3]
```

```python
import functools

import jax
import jax.numpy as jnp
from jax import lax
from jax.experimental import pallas as pl
from jax.experimental.pallas import tpu as pltpu
from jax.sharding import PartitionSpec as P

SIDE = 0.4
STEP = 0.1
THERMAL = 0.2
HALINE = 0.8
GRAVITY = 0.1
DRAG = 2.0
HIGH = lax.Precision.HIGHEST
UNROLL = 5


def levels_loop(levels, body, carry):
    unroll = UNROLL if levels % UNROLL == 0 else 1

    def group(index, carry):
        for step in range(unroll):
            carry = body(index * unroll + step, carry)
        return carry

    return lax.fori_loop(0, levels // unroll, group, carry)


def tile(k):
    return pl.ds(pl.multiple_of(8 * (k + 1), 8), 8)


def density(temp, salt):
    return HALINE * salt - THERMAL * temp


def tile_update(k, fields, above, below, around, wet, wet_v, wet_around, press, press_around, cor, bat):
    half_u, half_v = 0.5 * fields[2], 0.5 * fields[3]
    ways = (SIDE - half_u, SIDE + half_u, SIDE - half_v, SIDE + half_v)
    own = SIDE * wet_v
    for way, wet_n in zip(ways, wet_around):
        own = own + way * wet_n
    tend = []
    for f, up, down, sides in zip(fields, above, below, around):
        t = SIDE * (up + down) - own * f
        for way, q in zip(ways, sides):
            t = t + way * q
        tend.append(t)
    wet_e, wet_w, wet_n, wet_s = wet_around
    m_e, m_w, m_n, m_s = press_around
    gx = 0.5 * (m_e - m_w - press * (wet_e - wet_w))
    gy = 0.5 * (m_n - m_s - press * (wet_n - wet_s))
    rate = jnp.where(bat == k + 1, DRAG, 0.0)
    tend[2] = tend[2] + (cor * fields[3] - gx - rate * fields[2])
    tend[3] = tend[3] - (cor * fields[2] + gy + rate * fields[3])
    scale = STEP * wet
    return [f + scale * t for f, t in zip(fields, tend)]


def from_side(centre, other, way, to_u, to_v):
    scale = STEP * centre[4]
    wet_n = other[4]
    adds = [scale * (way * (other[i] - wet_n * centre[i])) for i in range(4)]
    push = (0.5 * scale) * (wet_n * (other[5] - centre[5]))
    if to_u:
        adds[2] = adds[2] + to_u * push
    if to_v:
        adds[3] = adds[3] + to_v * push
    return adds


def way_of(cell, side):
    if side == "east":
        return SIDE - 0.5 * cell[2]
    if side == "west":
        return SIDE + 0.5 * cell[2]
    if side == "north":
        return SIDE - 0.5 * cell[3]
    return SIDE + 0.5 * cell[3]


PUSH = {"east": (-1.0, 0.0), "west": (1.0, 0.0), "north": (0.0, -1.0), "south": (0.0, 1.0)}


def side_adds(cell, other, side):
    return from_side(cell, other, way_of(cell, side), *PUSH[side])


def iotas(shape=(8, 128)):
    return lax.broadcasted_iota(jnp.int32, shape, 0), lax.broadcasted_iota(jnp.int32, shape, 1)


def first_kernel(levels, place, temp, salt, east, north, sea, bat_ref, cor_ref,
                 part, wet_ref, xs, zb, on, off, state, press):
    lon_odd = place[0] % 2
    lat_odd = place[1] % 2
    sub, lane = iotas()
    bat, cor = bat_ref[...], cor_ref[...]
    zero = jnp.zeros((8, 128), jnp.float32)
    for i in range(4):
        for edge in (-1, levels):
            state[i, pl.ds(8 * (edge + 1), 8), :] = zero
    for edge in (-1, levels):
        wet_ref[pl.ds(8 * (edge + 1), 8), :] = zero

    def keep(k, columns, values):
        out = []
        here = lane == k
        for j, value in enumerate(values):
            out.append(jnp.where(here, pltpu.roll(value, k, 1), columns[2 * j]))
            out.append(jnp.where(here, pltpu.roll(value, k + 1, 1), columns[2 * j + 1]))
        return out

    def prepare(k, carry):
        total, columns = carry
        wet = jnp.where(k < bat, sea[k], 0).astype(jnp.float32)
        fields = [ref[k] * wet for ref in (temp, salt, east, north)]
        for i in range(4):
            state[i, tile(k), :] = fields[i]
        wet_ref[tile(k), :] = wet
        dens = density(fields[0], fields[1])
        total = total + dens
        p = GRAVITY * (total - 0.5 * dens)
        press[pl.ds(pl.multiple_of(8 * k, 8), 8), :] = p
        return total, keep(k, columns, fields + [wet, p])

    _, columns = levels_loop(levels, prepare, (zero, [zero] * 12))

    open_sides = (lane < 127, lane > 0, sub < 7, sub > 0)

    def beside(value):
        moved = (pltpu.roll(value, 127, 1), pltpu.roll(value, 1, 1), pltpu.roll(value, 7, 0), pltpu.roll(value, 1, 0))
        return [jnp.where(ok, m, 0.0) for ok, m in zip(open_sides, moved)]

    def partial(k, more):
        fields = [state[i, tile(k), :] for i in range(4)]
        above = [state[i, tile(k - 1), :] for i in range(4)]
        below = [state[i, tile(k + 1), :] for i in range(4)]
        wet = wet_ref[tile(k), :]
        wet_v = wet_ref[tile(k - 1), :] + wet_ref[tile(k + 1), :]
        p = press[pl.ds(pl.multiple_of(8 * k, 8), 8), :]
        new = tile_update(k, fields, above, below, [beside(f) for f in fields], wet, wet_v, beside(wet),
                          p, beside(wet * p), cor, bat)
        for i in range(4):
            part[i, tile(k), :] = new[i]
        return keep(k, more, new)

    more = levels_loop(levels, partial, [zero] * 8)
    for i in range(4):
        for edge in (-1, levels):
            part[i, pl.ds(8 * (edge + 1), 8), :] = zero

    for ref, row in ((xs, 7 - 7 * lat_odd), (zb, 7 * lat_odd)):
        rows = pl.ds(8 + row, levels, stride=8)
        planes = [state[i, rows, :] for i in range(4)] + [wet_ref[rows, :]] + [part[i, rows, :] for i in range(4)]
        for i, plane in enumerate(planes):
            ref[pl.ds(levels * i, levels), :] = plane
        left = ref.shape[0] - 9 * levels
        if left:
            ref[pl.ds(9 * levels, left), :] = jnp.zeros((left, 128), jnp.float32)
    columns = columns + more
    for j in range(10):
        west, eastern = columns[2 * j], columns[2 * j + 1]
        on[j] = jnp.where(lon_odd == 0, eastern, west)
        off[j] = jnp.where(lon_odd == 0, west, eastern)


def sides_of(lon_odd, on_own, off_own, on, off):
    odd = lon_odd == 1
    west = [jnp.where(odd, on_own[j], off_own[j]) for j in range(10)]
    east = [jnp.where(odd, off_own[j], on_own[j]) for j in range(10)]
    far_west = [jnp.where(odd, on[j], off[j]) for j in range(10)]
    far_east = [jnp.where(odd, off[j], on[j]) for j in range(10)]
    return west, east, far_west, far_east


def second_kernel(levels, place, part, on_own, off_own, on, off, full, corner_xs, corner_zb):
    lon_odd = place[0] % 2
    lat_odd = place[1] % 2
    sub, lane = iotas()
    west, east, far_west, far_east = sides_of(lon_odd, on_own, off_own, on, off)
    adds_w = side_adds(west[:6], far_west[:6], "west")
    adds_e = side_adds(east[:6], far_east[:6], "east")
    entries = far_west[:6] + adds_w + far_east[:6] + adds_e
    for ref, flag in ((corner_xs, lat_odd == 0), (corner_zb, lat_odd == 1)):
        for r, entry in enumerate(entries):
            ref[pl.ds(r, 1), :] = jnp.where(flag, entry[7:8, :], entry[0:1, :])
        ref[pl.ds(20, 4), :] = jnp.zeros((4, 128), jnp.float32)

    def add(k, carry):
        for i in range(4):
            extra_w = pltpu.roll(adds_w[i], 128 - k, 1)
            extra_e = pltpu.roll(adds_e[i], 127 - k, 1)
            extra = jnp.where(lane == 0, extra_w, jnp.where(lane == 127, extra_e, 0.0))
            full[i, tile(k), :] = part[i, tile(k), :] + extra
        return carry

    levels_loop(levels, add, 0)
    zero = jnp.zeros((8, 128), jnp.float32)
    for i in range(4):
        for edge in (-1, levels):
            full[i, pl.ds(8 * (edge + 1), 8), :] = zero


def third_kernel(levels, tops, place, full_in, wet_ref, bat_ref, cor_ref, xs_own, zb_own, xs, zb,
                 on_own, off_own, on, off, corner_xs, corner_zb,
                 temp, salt, east_out, north_out, full, halo, flipped):
    lon_odd = place[0] % 2
    lat_odd = place[1] % 2
    odd = lat_odd == 1
    top = place[1] == tops
    sub, lane = iotas()
    bat, cor = bat_ref[...], cor_ref[...]
    full[...] = full_in[...]

    south_c = jnp.where(odd, corner_xs[...], corner_zb[...])
    north_c = jnp.where(odd, corner_zb[...], corner_xs[...])
    r = lax.broadcasted_iota(jnp.int32, (24, 128), 0)
    swapped = jnp.concatenate([north_c[10:20], north_c[0:10], north_c[20:24]], axis=0)
    s = r % 10
    swapped = jnp.where((s == 2) | (s == 3) | (s == 8) | (s == 9), -swapped, swapped)
    north_c = jnp.where(top, swapped, north_c)

    west, east, far_west, far_east = sides_of(lon_odd, on_own, off_own, on, off)
    after = []
    for own, far, toward, base in ((west, far_west, "east", 0), (east, far_east, "west", 10)):
        new = list(far[6:10])
        south_cell = [south_c[base + i : base + i + 1, :] for i in range(6)]
        north_cell = [north_c[base + i : base + i + 1, :] for i in range(6)]
        for i, a in enumerate(side_adds(far[:6], own[:6], toward)):
            new[i] = new[i] + a
        for i, a in enumerate(side_adds(far[:6], south_cell, "south")):
            new[i] = new[i] + jnp.where(sub == 0, a, 0.0)
        for i, a in enumerate(side_adds(far[:6], north_cell, "north")):
            new[i] = new[i] + jnp.where(sub == 7, a, 0.0)
        after.append(new)
    row, col = iotas((128, 128))
    upper = jnp.where(row < col, 1.0, jnp.where(row == col, 0.5, 0.0))
    dens = jnp.concatenate([density(new[0], new[1]) for new in after], axis=0)
    p = GRAVITY * jnp.dot(dens, upper, precision=HIGH, preferred_element_type=jnp.float32)
    far_cols = []
    for j, (new, far) in enumerate(zip(after, (far_west, far_east))):
        far_cols.append(new + [far[4] * p[8 * j : 8 * j + 8], far[4]])

    @pl.when(jnp.logical_not(top))
    def _():
        flipped[...] = jnp.where(odd, zb[...], xs[...])

    @pl.when(top)
    def _():
        mirror = 127 - lax.broadcasted_iota(jnp.int32, (8, 128), 1)
        count = (9 * levels + 7) // 8

        def turn(t, carry):
            at = pl.ds(pl.multiple_of(8 * t, 8), 8)
            flipped[at, :] = jnp.take_along_axis(zb[at, :], mirror, axis=1, mode="promise_in_bounds")
            return carry

        lax.fori_loop(0, count, turn, 0)

    def plane(ref, i):
        return ref[pl.ds(levels * i, levels), :]

    sign = jnp.where(top, -1.0, 1.0)
    signs = [1.0, 1.0, sign, sign, 1.0, 1.0, 1.0, sign, sign]
    north_far = [plane(flipped, i) * signs[i] for i in range(9)]
    south_far = [jnp.where(odd, plane(xs, i), plane(zb, i)) for i in range(9)]
    north_own = [jnp.where(odd, plane(zb_own, i), plane(xs_own, i)) for i in range(5)]
    south_own = [jnp.where(odd, plane(xs_own, i), plane(zb_own, i)) for i in range(5)]
    row, col = iotas((levels, levels))
    lower = jnp.where(col < row, 1.0, jnp.where(row == col, 0.5, 0.0))

    def pressures(planes):
        dens = jnp.concatenate([density(f[0], f[1]) for f in planes], axis=1)
        p = GRAVITY * jnp.dot(lower, dens, precision=HIGH, preferred_element_type=jnp.float32)
        return [p[:, 128 * j : 128 * j + 128] for j in range(len(planes))]

    before = pressures([south_far, north_far, south_own, north_own])
    lanes = lax.broadcasted_iota(jnp.int32, (levels, 128), 1)
    corners = jnp.concatenate([south_c, north_c, jnp.zeros((80, 128), jnp.float32)], axis=0).T[:levels]
    results = []
    for n, (far, own, own_side, far_side, own_row) in enumerate(
        ((south_far, south_own, "south", "north", 0), (north_far, north_own, "north", "south", 7))
    ):
        far_cell = far[:5] + [before[n]]
        own_cell = own[:5] + [before[2 + n]]
        rows = pl.ds(8 + own_row, levels, stride=8)
        for i, a in enumerate(side_adds(own_cell, far_cell, own_side)):
            full[i, rows, :] = full[i, rows, :] + a
        new = []
        for i, a in enumerate(side_adds(far_cell, own_cell, far_side)):
            c = 24 * n + 6 + i
            extra = jnp.where(lanes == 0, corners[:, c : c + 1], 0.0)
            extra = jnp.where(lanes == 127, corners[:, c + 10 : c + 11], extra)
            new.append(far[5 + i] + a + extra)
        results.append(new)
    later = pressures(results)
    for n, (new, far) in enumerate(zip(results, (south_far, north_far))):
        for i, value in enumerate(new + [far[4] * later[n], far[4]]):
            halo[n, i, pl.ds(0, levels), :] = value

    def beside(value, k, j):
        far_e = pltpu.roll(far_cols[1][j], 127 - k, 1)
        far_w = pltpu.roll(far_cols[0][j], 128 - k, 1)
        return (
            jnp.where(lane == 127, far_e, pltpu.roll(value, 127, 1)),
            jnp.where(lane == 0, far_w, pltpu.roll(value, 1, 1)),
            jnp.where(sub == 7, halo[1, j, pl.ds(k, 1), :], pltpu.roll(value, 7, 0)),
            jnp.where(sub == 0, halo[0, j, pl.ds(k, 1), :], pltpu.roll(value, 1, 0)),
        )

    outs = (temp, salt, east_out, north_out)

    def last(k, total):
        fields = [full[i, tile(k), :] for i in range(4)]
        above = [full[i, tile(k - 1), :] for i in range(4)]
        below = [full[i, tile(k + 1), :] for i in range(4)]
        wet = wet_ref[tile(k), :]
        wet_v = wet_ref[tile(k - 1), :] + wet_ref[tile(k + 1), :]
        dens = density(fields[0], fields[1])
        total = total + dens
        p = GRAVITY * (total - 0.5 * dens)
        new = tile_update(k, fields, above, below, [beside(f, k, i) for i, f in enumerate(fields)], wet, wet_v,
                          beside(wet, k, 5), p, beside(wet * p, k, 4), cor, bat)
        for ref, value in zip(outs, new):
            ref[k] = value
        return total

    levels_loop(levels, last, jnp.zeros((8, 128), jnp.float32))


def shape(*dims):
    return jax.ShapeDtypeStruct(dims, jnp.float32)


def call(kernel, outs, ins, scratch=()):
    vmem = pl.BlockSpec(memory_space=pltpu.VMEM)
    return pl.pallas_call(
        kernel,
        out_shape=outs,
        in_specs=[pl.BlockSpec(memory_space=pltpu.SMEM)] + [vmem] * (len(ins) - 1),
        out_specs=[vmem] * len(outs),
        scratch_shapes=list(scratch),
        compiler_params=pltpu.CompilerParams(vmem_limit_bytes=40 * 2**20),
        cost_estimate=pl.CostEstimate(flops=10**7, bytes_accessed=4 * 10**6, transcendentals=0),
    )(*ins)


def pairs_of(names, count_lon, count_lat):
    def at(lon, lat):
        return lon * count_lat + lat if names[0] == "lon" else lat * count_lon + lon

    every = [(lon, lat) for lon in range(count_lon) for lat in range(count_lat)]
    on = [(at(o, a), at(o ^ 1, a)) for o, a in every]
    off = [(at(o, a), at((o + 1 if o % 2 else o - 1) % count_lon, a)) for o, a in every]
    xs = [(at(o, a), at(o, a ^ 1)) for o, a in every]
    zb = []
    for o, a in every:
        if a == count_lat - 1:
            zb.append((at(o, a), at(count_lon - 1 - o, a)))
        elif a > 0:
            zb.append((at(o, a), at(o, a + 1 if a % 2 else a - 1)))
    return on, off, xs, zb


def per_device(names, count_lon, count_lat, temp, salt, east, north, sea, bathymetry, vorticity):
    levels = temp.shape[0]
    on_pairs, off_pairs, xs_pairs, zb_pairs = pairs_of(names, count_lon, count_lat)
    place = jnp.stack([lax.axis_index("lon"), lax.axis_index("lat")]).astype(jnp.int32)
    tall = 8 * (levels + 2)
    ten = shape(10, 8, 128)
    long = 8 * ((9 * levels + 7) // 8)
    message = shape(long, 128)
    part, wet, xs_own, zb_own, on_own, off_own = call(
        functools.partial(first_kernel, levels),
        [shape(4, tall, 128), shape(tall, 128), message, message, ten, ten],
        [place, temp, salt, east, north, sea, bathymetry, vorticity],
        [pltpu.VMEM((4, tall, 128), jnp.float32), pltpu.VMEM((8 * levels, 128), jnp.float32)],
    )
    move = functools.partial(lax.ppermute, axis_name=names)
    xs = move(xs_own, perm=xs_pairs)
    on = move(on_own, perm=on_pairs)
    off = move(off_own, perm=off_pairs)
    zb = move(zb_own, perm=zb_pairs)
    full, corner_xs, corner_zb = call(
        functools.partial(second_kernel, levels),
        [shape(4, tall, 128), shape(24, 128), shape(24, 128)],
        [place, part, on_own, off_own, on, off],
    )
    corner_xs = move(corner_xs, perm=xs_pairs)
    corner_zb = move(corner_zb, perm=zb_pairs)
    out = shape(levels, 8, 128)
    return tuple(
        call(
            functools.partial(third_kernel, levels, count_lat - 1),
            [out] * 4,
            [place, full, wet, bathymetry, vorticity, xs_own, zb_own, xs, zb, on_own, off_own, on, off,
             corner_xs, corner_zb],
            [
                pltpu.VMEM((4, tall, 128), jnp.float32),
                pltpu.VMEM((2, 6, 8 * ((levels + 7) // 8), 128), jnp.float32),
                pltpu.VMEM((long, 128), jnp.float32),
            ],
        )
    )


def solution(mesh):
    cube, plane = P(None, "lat", "lon"), P("lat", "lon")
    names = tuple(n for n in mesh.axis_names if n in ("lon", "lat"))
    return jax.shard_map(
        functools.partial(per_device, names, mesh.shape["lon"], mesh.shape["lat"]),
        mesh=mesh,
        in_specs=(cube,) * 5 + (plane,) * 2,
        out_specs=(cube,) * 4,
        check_vma=False,
    )
```

```python
import functools

import jax
import jax.numpy as jnp
from jax import lax
from jax.experimental import pallas as pl
from jax.experimental.pallas import tpu as pltpu
from jax.sharding import PartitionSpec as P

SIDE = 0.4
STEP = 0.1
THERMAL = 0.2
HALINE = 0.8
GRAVITY = 0.1
DRAG = 2.0
HIGH = lax.Precision.HIGHEST
LOW = 64
UNROLL_A = 5
UNROLL_B = 4
UNROLL_C = 8
UNROLL_D = 4


def levels_loop(first, last, unroll, body, carry):
    count = (last - first) // unroll

    def group(index, carry):
        for step in range(unroll):
            carry = body(first + index * unroll + step, carry)
        return carry

    carry = lax.fori_loop(0, count, group, carry)
    for k in range(first + count * unroll, last):
        carry = body(k, carry)
    return carry


def tile(k):
    return pl.ds(pl.multiple_of(8 * (k + 1), 8), 8)


def density(temp, salt):
    return HALINE * salt - THERMAL * temp


def tile_update(k, fields, above, below, around, wet, wet_v, wet_around, press, press_around, cor, bat, base, half):
    signs = (-1.0, 1.0, -1.0, 1.0)
    speeds = (fields[2], fields[2], fields[3], fields[3])
    ways = [b + v * h if s > 0 else b - v * h for b, h, v, s in zip(base, half, speeds, signs)]
    own = SIDE * wet_v
    for way, wet_n in zip(ways, wet_around):
        own = own + way * wet_n
    tend = []
    for f, up, down, sides in zip(fields, above, below, around):
        t = SIDE * (up + down) - own * f
        for way, q in zip(ways, sides):
            t = t + way * q
        tend.append(t)
    slopes = [h * (m - press * w) for h, m, w in zip(half, press_around, wet_around)]
    rate = jnp.where(bat == lax.convert_element_type(k + 1, jnp.float32), DRAG, 0.0)
    tend[2] = tend[2] + (cor * fields[3] - (slopes[0] - slopes[1]) - rate * fields[2])
    tend[3] = tend[3] - (cor * fields[2] + (slopes[2] - slopes[3]) + rate * fields[3])
    scale = STEP * wet
    return [f + scale * t for f, t in zip(fields, tend)]


def from_side(centre, other, way, to_u, to_v):
    scale = STEP * centre[4]
    wet_n = other[4]
    adds = [scale * (way * (other[i] - wet_n * centre[i])) for i in range(4)]
    push = (0.5 * scale) * (wet_n * (other[5] - centre[5]))
    if to_u:
        adds[2] = adds[2] + to_u * push
    if to_v:
        adds[3] = adds[3] + to_v * push
    return adds


def way_of(cell, side):
    if side == "east":
        return SIDE - 0.5 * cell[2]
    if side == "west":
        return SIDE + 0.5 * cell[2]
    if side == "north":
        return SIDE - 0.5 * cell[3]
    return SIDE + 0.5 * cell[3]


PUSH = {"east": (-1.0, 0.0), "west": (1.0, 0.0), "north": (0.0, -1.0), "south": (0.0, 1.0)}


def side_adds(cell, other, side):
    return from_side(cell, other, way_of(cell, side), *PUSH[side])


def iotas(shape=(8, 128)):
    return lax.broadcasted_iota(jnp.int32, shape, 0), lax.broadcasted_iota(jnp.int32, shape, 1)


def swap(value):
    _, lane = iotas(value.shape)
    return jnp.where(lane % 2 == 0, pltpu.roll(value, 127, 1), pltpu.roll(value, 1, 1))


def level_of(lane, odd):
    return jnp.where(lane % 2 == odd, lane // 2, LOW + lane // 2)


def running(odd):
    row, col = iotas((128, 128))
    row, col = level_of(row, odd), level_of(col, odd)
    return jnp.where(row < col, 1.0, jnp.where(row == col, 0.5, 0.0))


def merged(west, east):
    _, lane = iotas()
    even = lane % 2 == 0
    return (
        [jnp.where(even, w, pltpu.roll(e, 126, 1)) for w, e in zip(west, east)],
        [jnp.where(even, e, w) for w, e in zip(west, east)],
    )


def turn_of(k, high):
    return (127 - 2 * (k - LOW)) if high else (128 - 2 * k)


def first_kernel(levels, place, fields_in, sea, columns_in,
                 part, wet_ref, on, off, state, press):
    lon_odd = place[0] % 2
    sub, lane = iotas()
    bat, cor = columns_in[0], columns_in[1]
    zero = jnp.zeros((8, 128), jnp.float32)
    for i in range(4):
        for edge in (-1, levels):
            state[i, pl.ds(8 * (edge + 1), 8), :] = zero
            part[i, pl.ds(8 * (edge + 1), 8), :] = zero
    for edge in (-1, levels):
        wet_ref[pl.ds(8 * (edge + 1), 8), :] = zero
    pair = lane // 2

    def keep(k, columns, values, high):
        at = k - LOW if high else k
        here = pair == at
        return [jnp.where(here, pltpu.roll(v, 2 * at + 1, 1), c) for c, v in zip(columns, values)]

    def prepare(high, k, carry):
        total, columns = carry
        wet = sea[k]
        fields = [fields_in[i, k] for i in range(4)]
        for i in range(4):
            state[i, tile(k), :] = fields[i]
        wet_ref[tile(k), :] = wet
        dens = density(fields[0], fields[1])
        total = total + dens
        p = GRAVITY * (total - 0.5 * dens)
        press[tile(k), :] = p
        return total, keep(k, columns, fields + [wet, p], high)

    def ranges(first, last):
        parts = [(first, min(last, LOW), False), (max(first, LOW), last, True)]
        return [p for p in parts if p[0] < p[1]]

    total = zero
    columns = {False: [zero] * 6, True: [zero] * 6}
    for first, last, high in ranges(0, levels):
        total, columns[high] = levels_loop(
            first, last, UNROLL_A, functools.partial(prepare, high), (total, columns[high]))

    open_sides = [ok.astype(jnp.float32) for ok in (lane < 127, lane > 0, sub < 7, sub > 0)]
    base = [SIDE * ok for ok in open_sides]
    half = [0.5 * ok for ok in open_sides]

    def beside(value):
        return (pltpu.roll(value, 127, 1), pltpu.roll(value, 1, 1), pltpu.roll(value, 7, 0), pltpu.roll(value, 1, 0))

    def partial(high, k, more):
        fields = [state[i, tile(k), :] for i in range(4)]
        above = [state[i, tile(k - 1), :] for i in range(4)]
        below = [state[i, tile(k + 1), :] for i in range(4)]
        wet = wet_ref[tile(k), :]
        wet_v = wet_ref[tile(k - 1), :] + wet_ref[tile(k + 1), :]
        p = press[tile(k), :]
        new = tile_update(k, fields, above, below, [beside(f) for f in fields], wet, wet_v, beside(wet),
                          p, beside(wet * p), cor, bat, base, half)
        for i in range(4):
            part[i, tile(k), :] = new[i]
        return keep(k, more, new, high)

    more = {False: [zero] * 4, True: [zero] * 4}
    for first, last, high in ranges(0, levels):
        more[high] = levels_loop(first, last, UNROLL_B, functools.partial(partial, high), more[high])

    even = lane % 2 == 0
    for j, (low, high) in enumerate(zip(columns[False] + more[False], columns[True] + more[True])):
        eastern = jnp.where(even, low, pltpu.roll(high, 1, 1))
        west = jnp.where(even, pltpu.roll(high, 127, 1), low)
        on[j] = jnp.where(lon_odd == 0, eastern, west)
        off[j] = jnp.where(lon_odd == 0, west, eastern)


def rows_kernel(levels, place, state, wet_ref, part, xs, zb):
    lat_odd = place[1] % 2
    for ref, row in ((xs, 7 - 7 * lat_odd), (zb, 7 * lat_odd)):
        rows = pl.ds(8 + row, levels, stride=8)
        planes = [state[i, rows, :] for i in range(4)] + [wet_ref[rows, :]] + [part[i, rows, :] for i in range(4)]
        for i, plane in enumerate(planes):
            ref[pl.ds(levels * i, levels), :] = plane
        left = ref.shape[0] - 9 * levels
        if left:
            ref[pl.ds(9 * levels, left), :] = jnp.zeros((left, 128), jnp.float32)


def sides_of(lon_odd, on_own, off_own, on, off):
    odd = lon_odd == 1
    west = [swap(jnp.where(odd, on_own[j], off_own[j])) for j in range(10)]
    east = [swap(jnp.where(odd, off_own[j], on_own[j])) for j in range(10)]
    far_west = [jnp.where(odd, on[j], off[j]) for j in range(10)]
    far_east = [jnp.where(odd, off[j], on[j]) for j in range(10)]
    return west, east, far_west, far_east


def second_kernel(levels, place, part, on_own, off_own, on, off, full, corner_xs, corner_zb):
    lon_odd = place[0] % 2
    lat_odd = place[1] % 2
    _, lane = iotas()
    west, east, far_west, far_east = sides_of(lon_odd, on_own, off_own, on, off)
    adds_w = side_adds(west[:6], far_west[:6], "west")
    adds_e = side_adds(east[:6], far_east[:6], "east")
    entries = far_west[:6] + adds_w + far_east[:6] + adds_e
    for ref, flag in ((corner_xs, lat_odd == 0), (corner_zb, lat_odd == 1)):
        for r, entry in enumerate(entries):
            ref[pl.ds(r, 1), :] = jnp.where(flag, entry[7:8, :], entry[0:1, :])
        ref[pl.ds(20, 4), :] = jnp.zeros((4, 128), jnp.float32)
    ends = (lane == 0) | (lane == 127)

    def add(extra, high, k, carry):
        for i in range(4):
            more = jnp.where(ends, pltpu.roll(extra[i], turn_of(k, high), 1), 0.0)
            full[i, tile(k), :] = part[i, tile(k), :] + more
        return carry

    low, high = merged(adds_w, adds_e)
    levels_loop(0, min(LOW, levels), UNROLL_C, functools.partial(add, low, False), 0)
    if levels > LOW:
        levels_loop(LOW, levels, UNROLL_C, functools.partial(add, high, True), 0)
    zero = jnp.zeros((8, 128), jnp.float32)
    for i in range(4):
        for edge in (-1, levels):
            full[i, pl.ds(8 * (edge + 1), 8), :] = zero


def third_kernel(levels, tops, place, full_in, wet_ref, columns_in, xs_own, zb_own, xs, zb,
                 on_own, off_own, on, off, corner_xs, corner_zb,
                 temp_hbm, salt_hbm, east_hbm, north_hbm, full, halo, flipped, turned, outs, sems):
    lon_odd = place[0] % 2
    lat_odd = place[1] % 2
    odd = lat_odd == 1
    top = place[1] == tops
    sub, lane = iotas()
    bat, cor = columns_in[0], columns_in[1]
    full[...] = full_in[...]

    south_c = jnp.where(odd, corner_xs[...], corner_zb[...])
    north_c = jnp.where(odd, corner_zb[...], corner_xs[...])
    r = lax.broadcasted_iota(jnp.int32, (24, 128), 0)
    swapped = swap(jnp.concatenate([north_c[10:20], north_c[0:10], north_c[20:24]], axis=0))
    s = r % 10
    swapped = jnp.where((s == 2) | (s == 3) | (s == 8) | (s == 9), -swapped, swapped)
    north_c = jnp.where(top, swapped, north_c)

    west, east, far_west, far_east = sides_of(lon_odd, on_own, off_own, on, off)
    far_cols = []
    for own, far, toward, base, order in ((west, far_west, "east", 0, 0), (east, far_east, "west", 10, 1)):
        new = list(far[6:10])
        south_cell = [south_c[base + i : base + i + 1, :] for i in range(6)]
        north_cell = [north_c[base + i : base + i + 1, :] for i in range(6)]
        for i, a in enumerate(side_adds(far[:6], own[:6], toward)):
            new[i] = new[i] + a
        for i, a in enumerate(side_adds(far[:6], south_cell, "south")):
            new[i] = new[i] + jnp.where(sub == 0, a, 0.0)
        for i, a in enumerate(side_adds(far[:6], north_cell, "north")):
            new[i] = new[i] + jnp.where(sub == 7, a, 0.0)
        p = GRAVITY * jnp.dot(density(new[0], new[1]), running(order), precision=HIGH,
                              preferred_element_type=jnp.float32)
        far_cols.append(new + [far[4] * p, far[4]])

    @pl.when(jnp.logical_not(top))
    def _():
        flipped[...] = jnp.where(odd, zb[...], xs[...])

    @pl.when(top)
    def _():
        mirror = 127 - lane
        for t in range(flipped.shape[0] // 8):
            at = pl.ds(8 * t, 8)
            flipped[at, :] = jnp.take_along_axis(zb[at, :], mirror, axis=1, mode="promise_in_bounds")

    def plane(ref, i):
        return ref[pl.ds(levels * i, levels), :]

    sign = jnp.where(top, -1.0, 1.0)
    signs = [1.0, 1.0, sign, sign, 1.0, 1.0, 1.0, sign, sign]
    north_far = [plane(flipped, i) * signs[i] for i in range(9)]
    south_far = [jnp.where(odd, plane(xs, i), plane(zb, i)) for i in range(9)]
    north_own = [jnp.where(odd, plane(zb_own, i), plane(xs_own, i)) for i in range(5)]
    south_own = [jnp.where(odd, plane(xs_own, i), plane(zb_own, i)) for i in range(5)]
    row, col = iotas((levels, levels))
    lower = jnp.where(col < row, 1.0, jnp.where(row == col, 0.5, 0.0))

    def pressures(planes):
        dens = jnp.concatenate([density(f[0], f[1]) for f in planes], axis=1)
        p = GRAVITY * jnp.dot(lower, dens, precision=HIGH, preferred_element_type=jnp.float32)
        return [p[:, 128 * j : 128 * j + 128] for j in range(len(planes))]

    before = pressures([south_far, north_far, south_own, north_own])
    lanes = lax.broadcasted_iota(jnp.int32, (levels, 128), 1)
    turned[...] = jnp.concatenate([south_c, north_c, jnp.zeros((80, 128), jnp.float32)], axis=0).T

    def in_order(odd_first):
        low = min(LOW, levels)
        parts = [turned[pl.ds(odd_first, low, stride=2), :]]
        if levels > LOW:
            parts.append(turned[pl.ds(1 - odd_first, levels - LOW, stride=2), :])
        return jnp.concatenate(parts, axis=0)

    west_c, east_c = in_order(0), in_order(1)
    results = []
    for n, (far, own, own_side, far_side, own_row) in enumerate(
        ((south_far, south_own, "south", "north", 0), (north_far, north_own, "north", "south", 7))
    ):
        far_cell = far[:5] + [before[n]]
        own_cell = own[:5] + [before[2 + n]]
        rows = pl.ds(8 + own_row, levels, stride=8)
        for i, a in enumerate(side_adds(own_cell, far_cell, own_side)):
            full[i, rows, :] = full[i, rows, :] + a
        new = []
        for i, a in enumerate(side_adds(far_cell, own_cell, far_side)):
            c = 24 * n + 6 + i
            extra = jnp.where(lanes == 0, west_c[:, c : c + 1], 0.0)
            extra = jnp.where(lanes == 127, east_c[:, c + 10 : c + 11], extra)
            new.append(far[5 + i] + a + extra)
        results.append(new)
    later = pressures(results)
    for n, (new, far) in enumerate(zip(results, (south_far, north_far))):
        for i, value in enumerate(new + [far[4] * later[n], far[4]]):
            halo[n, i, pl.ds(0, levels), :] = value

    chunk = 25 if levels % 25 == 0 else levels

    def copy_of(i, c):
        rows = pl.ds(c * chunk, chunk)
        target = (temp_hbm, salt_hbm, east_hbm, north_hbm)[i]
        return pltpu.make_async_copy(outs.at[i, rows], target.at[rows], sems.at[i, c])

    def beside(value, k, j, extra, high):
        far = pltpu.roll(extra[j], turn_of(k, high), 1)
        return (
            jnp.where(lane == 127, far, pltpu.roll(value, 127, 1)),
            jnp.where(lane == 0, far, pltpu.roll(value, 1, 1)),
            jnp.where(sub == 7, halo[1, j, pl.ds(k, 1), :], pltpu.roll(value, 7, 0)),
            jnp.where(sub == 0, halo[0, j, pl.ds(k, 1), :], pltpu.roll(value, 1, 0)),
        )

    base = [SIDE] * 4
    half = [0.5] * 4

    def last_step(extra, high, k, total):
        fields = [full[i, tile(k), :] for i in range(4)]
        above = [full[i, tile(k - 1), :] for i in range(4)]
        below = [full[i, tile(k + 1), :] for i in range(4)]
        wet = wet_ref[tile(k), :]
        wet_v = wet_ref[tile(k - 1), :] + wet_ref[tile(k + 1), :]
        dens = density(fields[0], fields[1])
        total = total + dens
        p = GRAVITY * (total - 0.5 * dens)
        new = tile_update(k, fields, above, below, [beside(f, k, i, extra, high) for i, f in enumerate(fields)],
                          wet, wet_v, beside(wet, k, 5, extra, high), p, beside(wet * p, k, 4, extra, high),
                          cor, bat, base, half)
        for i in range(4):
            outs[i, k] = new[i]
        return total

    extras = merged(far_cols[0], far_cols[1])
    total = jnp.zeros((8, 128), jnp.float32)
    for c in range(levels // chunk):
        first, last = c * chunk, (c + 1) * chunk
        for start, stop, high in ((first, min(last, LOW), False), (max(first, LOW), last, True)):
            if start < stop:
                total = levels_loop(start, stop, UNROLL_D, functools.partial(last_step, extras[int(high)], high), total)
        for i in range(4):
            copy_of(i, c).start()
    for c in range(levels // chunk):
        for i in range(4):
            copy_of(i, c).wait()


def shape(*dims):
    return jax.ShapeDtypeStruct(dims, jnp.float32)


def call(kernel, outs, ins, scratch=(), far_ins=(), far_outs=False):
    vmem = pl.BlockSpec(memory_space=pltpu.VMEM)
    hbm = pl.BlockSpec(memory_space=pltpu.HBM)
    return pl.pallas_call(
        kernel,
        out_shape=outs,
        in_specs=[pl.BlockSpec(memory_space=pltpu.SMEM)] + [hbm if i in far_ins else vmem for i in range(1, len(ins))],
        out_specs=[hbm if far_outs else vmem] * len(outs),
        scratch_shapes=list(scratch),
        compiler_params=pltpu.CompilerParams(vmem_limit_bytes=40 * 2**20),
        cost_estimate=pl.CostEstimate(flops=10**11, bytes_accessed=1000, transcendentals=0),
    )(*ins)


def pairs_of(names, count_lon, count_lat):
    def at(lon, lat):
        return lon * count_lat + lat if names[0] == "lon" else lat * count_lon + lon

    every = [(lon, lat) for lon in range(count_lon) for lat in range(count_lat)]
    on = [(at(o, a), at(o ^ 1, a)) for o, a in every]
    off = [(at(o, a), at((o + 1 if o % 2 else o - 1) % count_lon, a)) for o, a in every]
    xs = [(at(o, a), at(o, a ^ 1)) for o, a in every]
    zb = []
    for o, a in every:
        if a == count_lat - 1:
            zb.append((at(o, a), at(count_lon - 1 - o, a)))
        elif a > 0:
            zb.append((at(o, a), at(o, a + 1 if a % 2 else a - 1)))
    return on, off, xs, zb


def per_device(names, count_lon, count_lat, temp, salt, east, north, sea, bathymetry, vorticity):
    levels = temp.shape[0]
    on_pairs, off_pairs, xs_pairs, zb_pairs = pairs_of(names, count_lon, count_lat)
    place = jnp.stack([lax.axis_index("lon"), lax.axis_index("lat")]).astype(jnp.int32)
    tall = 8 * (levels + 2)
    ten = shape(10, 8, 128)
    long = 8 * ((9 * levels + 7) // 8)
    message = shape(long, 128)
    cube = (levels, 8, 128)
    chunks = 3 if levels % 25 == 0 else 1
    level_ids = lax.broadcasted_iota(jnp.int32, sea.shape, 0)
    wet_in = jnp.where(level_ids < bathymetry[None], sea, 0).astype(jnp.float32)
    fields = jnp.stack([temp, salt, east, north]) * wet_in
    columns = jnp.stack([bathymetry.astype(jnp.float32), vorticity])
    part, wet, on_own, off_own, state = call(
        functools.partial(first_kernel, levels),
        [shape(4, tall, 128), shape(tall, 128), ten, ten, shape(4, tall, 128)],
        [place, fields, wet_in, columns],
        [pltpu.VMEM((tall, 128), jnp.float32)],
    )
    move = functools.partial(lax.ppermute, axis_name=names)
    on = move(on_own, perm=on_pairs)
    off = move(off_own, perm=off_pairs)
    xs_own, zb_own = call(functools.partial(rows_kernel, levels), [message] * 2, [place, state, wet, part])
    xs = move(xs_own, perm=xs_pairs)
    zb = move(zb_own, perm=zb_pairs)
    full, corner_xs, corner_zb = call(
        functools.partial(second_kernel, levels),
        [shape(4, tall, 128), shape(24, 128), shape(24, 128)],
        [place, part, on_own, off_own, on, off],
    )
    corner_xs = move(corner_xs, perm=xs_pairs)
    corner_zb = move(corner_zb, perm=zb_pairs)
    out = shape(levels, 8, 128)
    return tuple(
        call(
            functools.partial(third_kernel, levels, count_lat - 1),
            [out] * 4,
            [place, full, wet, columns, xs_own, zb_own, xs, zb, on_own, off_own, on, off,
             corner_xs, corner_zb],
            [
                pltpu.VMEM((4, tall, 128), jnp.float32),
                pltpu.VMEM((2, 6, 8 * ((levels + 7) // 8), 128), jnp.float32),
                pltpu.VMEM((long, 128), jnp.float32),
                pltpu.VMEM((128, 128), jnp.float32),
                pltpu.VMEM((4,) + cube, jnp.float32),
                pltpu.SemaphoreType.DMA((4, chunks)),
            ],
            far_outs=True,
        )
    )


def solution(mesh):
    cube, plane = P(None, "lat", "lon"), P("lat", "lon")
    names = tuple(n for n in mesh.axis_names if n in ("lon", "lat"))
    return jax.shard_map(
        functools.partial(per_device, names, mesh.shape["lon"], mesh.shape["lat"]),
        mesh=mesh,
        in_specs=(cube,) * 5 + (plane,) * 2,
        out_specs=(cube,) * 4,
        check_vma=False,
    )
```

```python
import functools

import jax
import jax.numpy as jnp
from jax import lax
from jax.experimental import pallas as pl
from jax.experimental.pallas import tpu as pltpu
from jax.sharding import PartitionSpec as P

SIDE = 0.4
STEP = 0.1
THERMAL = 0.2
HALINE = 0.8
GRAVITY = 0.1
DRAG = 2.0
HIGH = lax.Precision.HIGHEST
LOW = 64
UNROLL_A = 5
UNROLL_B = 15
UNROLL_C = 16
UNROLL_D = 25
PART = 344
W_ROWS = 10**11
W_CORNER = 10**11
W_ADD = 10**12


def levels_loop(first, last, unroll, body, carry):
    count = (last - first) // unroll

    def group(index, carry):
        for step in range(unroll):
            carry = body(first + index * unroll + step, carry)
        return carry

    carry = lax.fori_loop(0, count, group, carry)
    for k in range(first + count * unroll, last):
        carry = body(k, carry)
    return carry


def tile(k):
    return pl.ds(pl.multiple_of(8 * (k + 1), 8), 8)


def density(temp, salt):
    return HALINE * salt - THERMAL * temp


def tile_update(k, fields, above, below, around, wet, wet_v, wet_around, press, press_around, cor, bat, base, half):
    signs = (-1.0, 1.0, -1.0, 1.0)
    speeds = (fields[2], fields[2], fields[3], fields[3])
    ways = [b + v * h if s > 0 else b - v * h for b, h, v, s in zip(base, half, speeds, signs)]
    own = SIDE * wet_v
    for way, wet_n in zip(ways, wet_around):
        own = own + way * wet_n
    tend = []
    for f, up, down, sides in zip(fields, above, below, around):
        t = SIDE * (up + down) - own * f
        for way, q in zip(ways, sides):
            t = t + way * q
        tend.append(t)
    slopes = [h * (m - press * w) for h, m, w in zip(half, press_around, wet_around)]
    rate = jnp.where(bat == lax.convert_element_type(k + 1, jnp.float32), DRAG, 0.0)
    tend[2] = tend[2] + (cor * fields[3] - (slopes[0] - slopes[1]) - rate * fields[2])
    tend[3] = tend[3] - (cor * fields[2] + (slopes[2] - slopes[3]) + rate * fields[3])
    scale = STEP * wet
    return [f + scale * t for f, t in zip(fields, tend)]


def from_side(centre, other, way, to_u, to_v):
    scale = STEP * centre[4]
    wet_n = other[4]
    adds = [scale * (way * (other[i] - wet_n * centre[i])) for i in range(4)]
    push = (0.5 * scale) * (wet_n * (other[5] - centre[5]))
    if to_u:
        adds[2] = adds[2] + to_u * push
    if to_v:
        adds[3] = adds[3] + to_v * push
    return adds


def way_of(cell, side):
    if side == "east":
        return SIDE - 0.5 * cell[2]
    if side == "west":
        return SIDE + 0.5 * cell[2]
    if side == "north":
        return SIDE - 0.5 * cell[3]
    return SIDE + 0.5 * cell[3]


PUSH = {"east": (-1.0, 0.0), "west": (1.0, 0.0), "north": (0.0, -1.0), "south": (0.0, 1.0)}


def side_adds(cell, other, side):
    return from_side(cell, other, way_of(cell, side), *PUSH[side])


def iotas(shape=(8, 128)):
    return lax.broadcasted_iota(jnp.int32, shape, 0), lax.broadcasted_iota(jnp.int32, shape, 1)


def swap(value):
    _, lane = iotas(value.shape)
    return jnp.where(lane % 2 == 0, pltpu.roll(value, 127, 1), pltpu.roll(value, 1, 1))


def level_of(lane, odd):
    return jnp.where(lane % 2 == odd, lane // 2, LOW + lane // 2)


def running(odd):
    row, col = iotas((128, 128))
    row, col = level_of(row, odd), level_of(col, odd)
    return jnp.where(row < col, 1.0, jnp.where(row == col, 0.5, 0.0))


def merged(west, east):
    _, lane = iotas()
    even = lane % 2 == 0
    return (
        [jnp.where(even, w, pltpu.roll(e, 126, 1)) for w, e in zip(west, east)],
        [jnp.where(even, e, w) for w, e in zip(west, east)],
    )


def turn_of(k, high):
    return (127 - 2 * (k - LOW)) if high else (128 - 2 * k)


def first_kernel(levels, place, temp_hbm, salt_hbm, east_hbm, north_hbm, sea_hbm, bat_hbm, cor_hbm,
                 part, wet_ref, on, off, state, planes, press, temp, salt, east, north, sea, bat_ref, sems, plane_sems):
    chunk = 25 if levels % 25 == 0 else levels
    chunks = levels // chunk
    inputs = ((temp_hbm, temp), (salt_hbm, salt), (east_hbm, east), (north_hbm, north), (sea_hbm, sea))

    def copy_of(i, c):
        source, target = inputs[i]
        rows = pl.ds(c * chunk, chunk)
        return pltpu.make_async_copy(source.at[rows], target.at[rows], sems.at[i, c])

    plane_copies = [
        pltpu.make_async_copy(bat_hbm, bat_ref, plane_sems.at[0]),
        pltpu.make_async_copy(cor_hbm, planes.at[1], plane_sems.at[1]),
    ]
    for copy in plane_copies:
        copy.start()
    for c in range(chunks):
        for i in range(5):
            copy_of(i, c).start()
    lon_odd = place[0] % 2
    sub, lane = iotas()
    zero = jnp.zeros((8, 128), jnp.float32)
    for i in range(4):
        for edge in (-1, levels):
            state[i, pl.ds(8 * (edge + 1), 8), :] = zero
            part[i, pl.ds(8 * (edge + 1), 8), :] = zero
    for edge in (-1, levels):
        wet_ref[pl.ds(8 * (edge + 1), 8), :] = zero
    for copy in plane_copies:
        copy.wait()
    depth = bat_ref[...]
    bat = depth.astype(jnp.float32)
    planes[0] = bat
    cor = planes[1]

    def prepare(k, total):
        wet = jnp.where(k < depth, sea[k], 0).astype(jnp.float32)
        fields = [ref[k] * wet for ref in (temp, salt, east, north)]
        for i in range(4):
            state[i, tile(k), :] = fields[i]
        wet_ref[tile(k), :] = wet
        dens = density(fields[0], fields[1])
        total = total + dens
        press[tile(k), :] = GRAVITY * (total - 0.5 * dens)
        return total

    total = zero
    for c in range(chunks):
        for i in range(5):
            copy_of(i, c).wait()
        total = levels_loop(c * chunk, (c + 1) * chunk, UNROLL_A, prepare, total)

    open_sides = [ok.astype(jnp.float32) for ok in (lane < 127, lane > 0, sub < 7, sub > 0)]
    base = [SIDE * ok for ok in open_sides]
    half = [0.5 * ok for ok in open_sides]

    def beside(value):
        return (pltpu.roll(value, 127, 1), pltpu.roll(value, 1, 1), pltpu.roll(value, 7, 0), pltpu.roll(value, 1, 0))

    def partial(k, carry):
        fields = [state[i, tile(k), :] for i in range(4)]
        above = [state[i, tile(k - 1), :] for i in range(4)]
        below = [state[i, tile(k + 1), :] for i in range(4)]
        wet = wet_ref[tile(k), :]
        wet_v = wet_ref[tile(k - 1), :] + wet_ref[tile(k + 1), :]
        p = press[tile(k), :]
        new = tile_update(k, fields, above, below, [beside(f) for f in fields], wet, wet_v, beside(wet),
                          p, beside(wet * p), cor, bat, base, half)
        for i in range(4):
            part[i, tile(k), :] = new[i]
        return carry

    levels_loop(0, levels, UNROLL_B, partial, 0)

    pair = lane // 2
    packed = {}
    for first, last in ((0, min(LOW, levels)), (LOW, levels)):
        columns = [zero] * 10
        for k in range(first, last):
            here = pair == k - first
            at = pl.ds(8 * (k + 1), 8)
            values = [state[i, at, :] for i in range(4)] + [wet_ref[at, :], press[at, :]]
            values = values + [part[i, at, :] for i in range(4)]
            columns = [jnp.where(here, pltpu.roll(v, 2 * (k - first) + 1, 1), c) for v, c in zip(values, columns)]
        packed[first] = columns
    even = lane % 2 == 0
    for j, (low, high) in enumerate(zip(packed[0], packed[LOW])):
        eastern = jnp.where(even, low, pltpu.roll(high, 1, 1))
        west = jnp.where(even, pltpu.roll(high, 127, 1), low)
        on[j] = jnp.where(lon_odd == 0, eastern, west)
        off[j] = jnp.where(lon_odd == 0, west, eastern)


def write_rows(levels, ref, row, state, wet_ref, part):
    rows = pl.ds(8 + row, levels, stride=8)
    planes = [state[i, rows, :] for i in range(4)] + [wet_ref[rows, :]] + [part[i, rows, :] for i in range(4)]
    for i, plane in enumerate(planes):
        ref[pl.ds(levels * i, levels), :] = plane
    left = long_of(levels) - 9 * levels
    if left:
        ref[pl.ds(9 * levels, left), :] = jnp.zeros((left, 128), jnp.float32)


def long_of(levels):
    return 8 * ((9 * levels + 7) // 8)


def rows_kernel(levels, tops, place, state, wet_ref, part, xs, fold_a):
    lat_odd = place[1] % 2
    write_rows(levels, xs, 7 - 7 * lat_odd, state, wet_ref, part)

    @pl.when(place[1] == tops)
    def _():
        rows = pl.ds(8 + 7, levels, stride=8)
        planes = [state[i, rows, :] for i in range(4)] + [wet_ref[rows, :]]
        for i, plane in enumerate(planes):
            count = min(levels, PART - levels * i)
            fold_a[pl.ds(levels * i, count), :] = plane[:count]


def sides_of(lon_odd, on_own, off_own, on, off):
    odd = lon_odd == 1
    west = [swap(jnp.where(odd, on_own[j], off_own[j])) for j in range(10)]
    east = [swap(jnp.where(odd, off_own[j], on_own[j])) for j in range(10)]
    far_west = [jnp.where(odd, on[j], off[j]) for j in range(10)]
    far_east = [jnp.where(odd, off[j], on[j]) for j in range(10)]
    return west, east, far_west, far_east


def corner_kernel(levels, tops, place, on_own, off_own, on, off, state, wet_ref, part, xs_own, zb, fold_b, corner_xs, extra):
    lon_odd = place[0] % 2
    lat_odd = place[1] % 2
    write_rows(levels, zb, 7 * lat_odd, state, wet_ref, part)
    west, east, far_west, far_east = sides_of(lon_odd, on_own, off_own, on, off)
    adds_w = side_adds(west[:6], far_west[:6], "west")
    adds_e = side_adds(east[:6], far_east[:6], "east")
    entries = far_west[:6] + adds_w + far_east[:6] + adds_e
    for ref, start, flag in ((corner_xs, 0, lat_odd == 0), (zb, long_of(levels), lat_odd == 1)):
        for r, entry in enumerate(entries):
            ref[pl.ds(start + r, 1), :] = jnp.where(flag, entry[7:8, :], entry[0:1, :])
        ref[pl.ds(start + 20, 4), :] = jnp.zeros((4, 128), jnp.float32)
    low, high = merged(adds_w, adds_e)
    for i in range(4):
        extra[i] = low[i]
        extra[4 + i] = high[i]

    @pl.when(place[1] == tops)
    def _():
        fold_b[...] = zb[pl.ds(PART, zb.shape[0] - PART), :]


def second_kernel(levels, place, part, extra, xs, fold_a, full):
    _, lane = iotas()
    ends = (lane == 0) | (lane == 127)

    def add(extra, high, k, carry):
        for i in range(4):
            more = jnp.where(ends, pltpu.roll(extra[i], turn_of(k, high), 1), 0.0)
            full[i, tile(k), :] = part[i, tile(k), :] + more
        return carry

    levels_loop(0, min(LOW, levels), UNROLL_C, functools.partial(add, [extra[i] for i in range(4)], False), 0)
    if levels > LOW:
        levels_loop(LOW, levels, UNROLL_C, functools.partial(add, [extra[4 + i] for i in range(4)], True), 0)
    zero = jnp.zeros((8, 128), jnp.float32)
    for i in range(4):
        for edge in (-1, levels):
            full[i, pl.ds(8 * (edge + 1), 8), :] = zero


def third_kernel(levels, tops, place, full_in, wet_ref, columns_in, xs_own, zb_own, xs, zb, fold_a, fold_b,
                 on_own, off_own, on, off, corner_xs,
                 temp_hbm, salt_hbm, east_hbm, north_hbm, full, halo, flipped, turned, outs, sems):
    lon_odd = place[0] % 2
    lat_odd = place[1] % 2
    odd = lat_odd == 1
    top = place[1] == tops
    sub, lane = iotas()
    bat, cor = columns_in[0], columns_in[1]
    full[...] = full_in[...]

    at_end = pl.ds(long_of(levels), 24)
    south_c = jnp.where(odd, corner_xs[...], zb[at_end, :])
    north_c = jnp.where(odd, jnp.where(top, fold_b[pl.ds(long_of(levels) - PART, 24), :], zb[at_end, :]), corner_xs[...])
    r = lax.broadcasted_iota(jnp.int32, (24, 128), 0)
    swapped = swap(jnp.concatenate([north_c[10:20], north_c[0:10], north_c[20:24]], axis=0))
    s = r % 10
    swapped = jnp.where((s == 2) | (s == 3) | (s == 8) | (s == 9), -swapped, swapped)
    north_c = jnp.where(top, swapped, north_c)

    west, east, far_west, far_east = sides_of(lon_odd, on_own, off_own, on, off)
    far_cols = []
    for own, far, toward, base, order in ((west, far_west, "east", 0, 0), (east, far_east, "west", 10, 1)):
        new = list(far[6:10])
        south_cell = [south_c[base + i : base + i + 1, :] for i in range(6)]
        north_cell = [north_c[base + i : base + i + 1, :] for i in range(6)]
        for i, a in enumerate(side_adds(far[:6], own[:6], toward)):
            new[i] = new[i] + a
        for i, a in enumerate(side_adds(far[:6], south_cell, "south")):
            new[i] = new[i] + jnp.where(sub == 0, a, 0.0)
        for i, a in enumerate(side_adds(far[:6], north_cell, "north")):
            new[i] = new[i] + jnp.where(sub == 7, a, 0.0)
        p = GRAVITY * jnp.dot(density(new[0], new[1]), running(order), precision=HIGH,
                              preferred_element_type=jnp.float32)
        far_cols.append(new + [far[4] * p, far[4]])

    @pl.when(jnp.logical_not(top))
    def _():
        flipped[...] = jnp.where(odd, zb[pl.ds(0, long_of(levels)), :], xs[...])

    @pl.when(top)
    def _():
        mirror = 127 - lane
        for t in range(flipped.shape[0] // 8):
            at = 8 * t
            rows = fold_a[pl.ds(at, 8), :] if at < PART else fold_b[pl.ds(at - PART, 8), :]
            flipped[pl.ds(at, 8), :] = jnp.take_along_axis(rows, mirror, axis=1, mode="promise_in_bounds")

    def plane(ref, i):
        return ref[pl.ds(levels * i, levels), :]

    sign = jnp.where(top, -1.0, 1.0)
    signs = [1.0, 1.0, sign, sign, 1.0, 1.0, 1.0, sign, sign]
    north_far = [plane(flipped, i) * signs[i] for i in range(9)]
    south_far = [jnp.where(odd, plane(xs, i), plane(zb, i)) for i in range(9)]
    north_own = [jnp.where(odd, plane(zb_own, i), plane(xs_own, i)) for i in range(5)]
    south_own = [jnp.where(odd, plane(xs_own, i), plane(zb_own, i)) for i in range(5)]
    row, col = iotas((levels, levels))
    lower = jnp.where(col < row, 1.0, jnp.where(row == col, 0.5, 0.0))

    def pressures(planes):
        dens = jnp.concatenate([density(f[0], f[1]) for f in planes], axis=1)
        p = GRAVITY * jnp.dot(lower, dens, precision=HIGH, preferred_element_type=jnp.float32)
        return [p[:, 128 * j : 128 * j + 128] for j in range(len(planes))]

    before = pressures([south_far, north_far, south_own, north_own])
    lanes = lax.broadcasted_iota(jnp.int32, (levels, 128), 1)
    turned[...] = jnp.concatenate([south_c, north_c, jnp.zeros((80, 128), jnp.float32)], axis=0).T

    def in_order(odd_first):
        low = min(LOW, levels)
        parts = [turned[pl.ds(odd_first, low, stride=2), :]]
        if levels > LOW:
            parts.append(turned[pl.ds(1 - odd_first, levels - LOW, stride=2), :])
        return jnp.concatenate(parts, axis=0)

    west_c, east_c = in_order(0), in_order(1)
    results = []
    for n, (far, own, own_side, far_side, own_row) in enumerate(
        ((south_far, south_own, "south", "north", 0), (north_far, north_own, "north", "south", 7))
    ):
        far_cell = far[:5] + [before[n]]
        own_cell = own[:5] + [before[2 + n]]
        rows = pl.ds(8 + own_row, levels, stride=8)
        for i, a in enumerate(side_adds(own_cell, far_cell, own_side)):
            full[i, rows, :] = full[i, rows, :] + a
        new = []
        for i, a in enumerate(side_adds(far_cell, own_cell, far_side)):
            c = 24 * n + 6 + i
            extra = jnp.where(lanes == 0, west_c[:, c : c + 1], 0.0)
            extra = jnp.where(lanes == 127, east_c[:, c + 10 : c + 11], extra)
            new.append(far[5 + i] + a + extra)
        results.append(new)
    later = pressures(results)
    for n, (new, far) in enumerate(zip(results, (south_far, north_far))):
        for i, value in enumerate(new + [far[4] * later[n], far[4]]):
            halo[n, i, pl.ds(0, levels), :] = value

    chunk = 25 if levels % 25 == 0 else levels

    def copy_of(i, c):
        rows = pl.ds(c * chunk, chunk)
        target = (temp_hbm, salt_hbm, east_hbm, north_hbm)[i]
        return pltpu.make_async_copy(outs.at[i, rows], target.at[rows], sems.at[i, c])

    def beside(value, k, j, extra, high):
        far = pltpu.roll(extra[j], turn_of(k, high), 1)
        return (
            jnp.where(lane == 127, far, pltpu.roll(value, 127, 1)),
            jnp.where(lane == 0, far, pltpu.roll(value, 1, 1)),
            jnp.where(sub == 7, halo[1, j, pl.ds(k, 1), :], pltpu.roll(value, 7, 0)),
            jnp.where(sub == 0, halo[0, j, pl.ds(k, 1), :], pltpu.roll(value, 1, 0)),
        )

    base = [SIDE] * 4
    half = [0.5] * 4

    def last_step(extra, high, k, total):
        fields = [full[i, tile(k), :] for i in range(4)]
        above = [full[i, tile(k - 1), :] for i in range(4)]
        below = [full[i, tile(k + 1), :] for i in range(4)]
        wet = wet_ref[tile(k), :]
        wet_v = wet_ref[tile(k - 1), :] + wet_ref[tile(k + 1), :]
        dens = density(fields[0], fields[1])
        total = total + dens
        p = GRAVITY * (total - 0.5 * dens)
        new = tile_update(k, fields, above, below, [beside(f, k, i, extra, high) for i, f in enumerate(fields)],
                          wet, wet_v, beside(wet, k, 5, extra, high), p, beside(wet * p, k, 4, extra, high),
                          cor, bat, base, half)
        for i in range(4):
            outs[i, k] = new[i]
        return total

    extras = merged(far_cols[0], far_cols[1])
    total = jnp.zeros((8, 128), jnp.float32)
    for c in range(levels // chunk):
        first, last = c * chunk, (c + 1) * chunk
        for start, stop, high in ((first, min(last, LOW), False), (max(first, LOW), last, True)):
            if start < stop:
                total = levels_loop(start, stop, UNROLL_D, functools.partial(last_step, extras[int(high)], high), total)
        for i in range(4):
            copy_of(i, c).start()
    for c in range(levels // chunk):
        for i in range(4):
            copy_of(i, c).wait()


def shape(*dims):
    return jax.ShapeDtypeStruct(dims, jnp.float32)


def call(kernel, outs, ins, scratch=(), far_ins=(), far_outs=False, work=10**11):
    vmem = pl.BlockSpec(memory_space=pltpu.VMEM)
    hbm = pl.BlockSpec(memory_space=pltpu.HBM)
    return pl.pallas_call(
        kernel,
        out_shape=outs,
        in_specs=[pl.BlockSpec(memory_space=pltpu.SMEM)] + [hbm if i in far_ins else vmem for i in range(1, len(ins))],
        out_specs=[hbm if far_outs else vmem] * len(outs),
        scratch_shapes=list(scratch),
        compiler_params=pltpu.CompilerParams(vmem_limit_bytes=20 * 2**20),
        cost_estimate=pl.CostEstimate(flops=work, bytes_accessed=1000, transcendentals=0),
    )(*ins)


def pairs_of(names, count_lon, count_lat):
    def at(lon, lat):
        return lon * count_lat + lat if names[0] == "lon" else lat * count_lon + lon

    every = [(lon, lat) for lon in range(count_lon) for lat in range(count_lat)]
    on = [(at(o, a), at(o ^ 1, a)) for o, a in every]
    off = [(at(o, a), at((o + 1 if o % 2 else o - 1) % count_lon, a)) for o, a in every]
    xs = [(at(o, a), at(o, a ^ 1)) for o, a in every]
    zb = [(at(o, a), at(o, a + 1 if a % 2 else a - 1)) for o, a in every if 0 < a < count_lat - 1]
    top = count_lat - 1
    to_relay = [(at(o, top), at(count_lon - 1 - o, top - 1)) for o in range(count_lon)]
    from_relay = [(at(o, top - 1), at(o, top)) for o in range(count_lon)]
    return on, off, xs, zb, to_relay, from_relay


def per_device(names, count_lon, count_lat, temp, salt, east, north, sea, bathymetry, vorticity):
    levels = temp.shape[0]
    on_pairs, off_pairs, xs_pairs, zb_pairs, to_relay, from_relay = pairs_of(names, count_lon, count_lat)
    place = jnp.stack([lax.axis_index("lon"), lax.axis_index("lat")]).astype(jnp.int32)
    tall = 8 * (levels + 2)
    ten = shape(10, 8, 128)
    long = long_of(levels)
    message = shape(long, 128)
    cube = (levels, 8, 128)
    chunks = 3 if levels % 25 == 0 else 1
    raw = [pltpu.with_memory_space_constraint(x, pltpu.HBM) for x in (temp, salt, east, north, sea, bathymetry, vorticity)]
    part, wet, on_own, off_own, state, columns = call(
        functools.partial(first_kernel, levels),
        [shape(4, tall, 128), shape(tall, 128), ten, ten, shape(4, tall, 128), shape(2, 8, 128)],
        [place, *raw],
        [pltpu.VMEM((tall, 128), jnp.float32)] + [pltpu.VMEM(cube, jnp.float32)] * 4
        + [pltpu.VMEM(cube, jnp.int32), pltpu.VMEM((8, 128), jnp.int32), pltpu.SemaphoreType.DMA((5, chunks)),
           pltpu.SemaphoreType.DMA((2,))],
        far_ins=(1, 2, 3, 4, 5, 6, 7),
    )
    move = functools.partial(lax.ppermute, axis_name=names)
    on = move(on_own, perm=on_pairs)
    off = move(off_own, perm=off_pairs)
    xs_own, fold_a = call(
        functools.partial(rows_kernel, levels, count_lat - 1),
        [message, shape(PART, 128)],
        [place, state, wet, part],
        work=W_ROWS,
    )
    fold_a = move(fold_a, perm=to_relay)
    xs = move(xs_own, perm=xs_pairs)
    zb_own, fold_b, corner_xs, extra = call(
        functools.partial(corner_kernel, levels, count_lat - 1),
        [shape(long + 24, 128), shape(long + 24 - PART, 128), shape(24, 128), shape(8, 8, 128)],
        [place, on_own, off_own, on, off, state, wet, part, xs_own],
        work=W_CORNER,
    )
    fold_b = move(fold_b, perm=to_relay)
    zb = move(zb_own, perm=zb_pairs)
    corner_xs = move(corner_xs, perm=xs_pairs)
    fold_a = move(fold_a, perm=from_relay)
    fold_b = move(fold_b, perm=from_relay)
    full, = call(functools.partial(second_kernel, levels), [shape(4, tall, 128)], [place, part, extra, xs, fold_a], work=W_ADD)
    out = shape(levels, 8, 128)
    return tuple(
        call(
            functools.partial(third_kernel, levels, count_lat - 1),
            [out] * 4,
            [place, full, wet, columns, xs_own, zb_own, xs, zb, fold_a, fold_b, on_own, off_own, on, off,
             corner_xs],
            [
                pltpu.VMEM((4, tall, 128), jnp.float32),
                pltpu.VMEM((2, 6, 8 * ((levels + 7) // 8), 128), jnp.float32),
                pltpu.VMEM((long, 128), jnp.float32),
                pltpu.VMEM((128, 128), jnp.float32),
                pltpu.VMEM((4,) + cube, jnp.float32),
                pltpu.SemaphoreType.DMA((4, chunks)),
            ],
            far_outs=True,
        )
    )


def solution(mesh):
    cube, plane = P(None, "lat", "lon"), P("lat", "lon")
    names = tuple(n for n in mesh.axis_names if n in ("lon", "lat"))
    return jax.shard_map(
        functools.partial(per_device, names, mesh.shape["lon"], mesh.shape["lat"]),
        mesh=mesh,
        in_specs=(cube,) * 5 + (plane,) * 2,
        out_specs=(cube,) * 4,
        check_vma=False,
    )
```

```python
import functools

import jax
import jax.numpy as jnp
from jax import lax
from jax.experimental import pallas as pl
from jax.experimental.pallas import tpu as pltpu
from jax.sharding import PartitionSpec as P

SIDE = 0.4
STEP = 0.1
THERMAL = 0.2
HALINE = 0.8
GRAVITY = 0.1
DRAG = 2.0
HIGH = lax.Precision.HIGHEST
LOW = 64
UNROLL_A = 5
UNROLL_B = 15
UNROLL_C = 16
UNROLL_D = 25
PART = 344
W_ROWS = 10**11
W_CORNER = 10**11
W_ADD = 10**11
W_CHOOSE = 10**12


def levels_loop(first, last, unroll, body, carry):
    count = (last - first) // unroll

    def group(index, carry):
        for step in range(unroll):
            carry = body(first + index * unroll + step, carry)
        return carry

    carry = lax.fori_loop(0, count, group, carry)
    for k in range(first + count * unroll, last):
        carry = body(k, carry)
    return carry


def tile(k):
    return pl.ds(pl.multiple_of(8 * (k + 1), 8), 8)


def density(temp, salt):
    return HALINE * salt - THERMAL * temp


def tile_update(k, fields, above, below, around, wet, wet_v, wet_around, press, press_around, cor, bat, base, half):
    signs = (-1.0, 1.0, -1.0, 1.0)
    speeds = (fields[2], fields[2], fields[3], fields[3])
    ways = [b + v * h if s > 0 else b - v * h for b, h, v, s in zip(base, half, speeds, signs)]
    own = SIDE * wet_v
    for way, wet_n in zip(ways, wet_around):
        own = own + way * wet_n
    tend = []
    for f, up, down, sides in zip(fields, above, below, around):
        t = SIDE * (up + down) - own * f
        for way, q in zip(ways, sides):
            t = t + way * q
        tend.append(t)
    slopes = [h * (m - press * w) for h, m, w in zip(half, press_around, wet_around)]
    rate = jnp.where(bat == lax.convert_element_type(k + 1, jnp.float32), DRAG, 0.0)
    tend[2] = tend[2] + (cor * fields[3] - (slopes[0] - slopes[1]) - rate * fields[2])
    tend[3] = tend[3] - (cor * fields[2] + (slopes[2] - slopes[3]) + rate * fields[3])
    scale = STEP * wet
    return [f + scale * t for f, t in zip(fields, tend)]


def from_side(centre, other, way, to_u, to_v):
    scale = STEP * centre[4]
    wet_n = other[4]
    adds = [scale * (way * (other[i] - wet_n * centre[i])) for i in range(4)]
    push = (0.5 * scale) * (wet_n * (other[5] - centre[5]))
    if to_u:
        adds[2] = adds[2] + to_u * push
    if to_v:
        adds[3] = adds[3] + to_v * push
    return adds


def way_of(cell, side):
    if side == "east":
        return SIDE - 0.5 * cell[2]
    if side == "west":
        return SIDE + 0.5 * cell[2]
    if side == "north":
        return SIDE - 0.5 * cell[3]
    return SIDE + 0.5 * cell[3]


PUSH = {"east": (-1.0, 0.0), "west": (1.0, 0.0), "north": (0.0, -1.0), "south": (0.0, 1.0)}


def side_adds(cell, other, side):
    return from_side(cell, other, way_of(cell, side), *PUSH[side])


def iotas(shape=(8, 128)):
    return lax.broadcasted_iota(jnp.int32, shape, 0), lax.broadcasted_iota(jnp.int32, shape, 1)


def swap(value):
    _, lane = iotas(value.shape)
    return jnp.where(lane % 2 == 0, pltpu.roll(value, 127, 1), pltpu.roll(value, 1, 1))


def level_of(lane, odd):
    return jnp.where(lane % 2 == odd, lane // 2, LOW + lane // 2)


def running(odd):
    row, col = iotas((128, 128))
    row, col = level_of(row, odd), level_of(col, odd)
    return jnp.where(row < col, 1.0, jnp.where(row == col, 0.5, 0.0))


def merged(west, east):
    _, lane = iotas()
    even = lane % 2 == 0
    return (
        [jnp.where(even, w, pltpu.roll(e, 126, 1)) for w, e in zip(west, east)],
        [jnp.where(even, e, w) for w, e in zip(west, east)],
    )


def turn_of(k, high):
    return (127 - 2 * (k - LOW)) if high else (128 - 2 * k)


def first_kernel(levels, place, temp_hbm, salt_hbm, east_hbm, north_hbm, sea_hbm, bat_hbm, cor_hbm,
                 part, wet_ref, on, off, state, planes, press, temp, salt, east, north, sea, bat_ref, sems, plane_sems):
    chunk = 25 if levels % 25 == 0 else levels
    chunks = levels // chunk
    inputs = ((temp_hbm, temp), (salt_hbm, salt), (east_hbm, east), (north_hbm, north), (sea_hbm, sea))

    def copy_of(i, c):
        source, target = inputs[i]
        rows = pl.ds(c * chunk, chunk)
        return pltpu.make_async_copy(source.at[rows], target.at[rows], sems.at[i, c])

    plane_copies = [
        pltpu.make_async_copy(bat_hbm, bat_ref, plane_sems.at[0]),
        pltpu.make_async_copy(cor_hbm, planes.at[1], plane_sems.at[1]),
    ]
    for copy in plane_copies:
        copy.start()
    for c in range(chunks):
        for i in range(5):
            copy_of(i, c).start()
    lon_odd = place[0] % 2
    sub, lane = iotas()
    zero = jnp.zeros((8, 128), jnp.float32)
    for i in range(4):
        for edge in (-1, levels):
            state[i, pl.ds(8 * (edge + 1), 8), :] = zero
            part[i, pl.ds(8 * (edge + 1), 8), :] = zero
    for edge in (-1, levels):
        wet_ref[pl.ds(8 * (edge + 1), 8), :] = zero
    for copy in plane_copies:
        copy.wait()
    depth = bat_ref[...]
    bat = depth.astype(jnp.float32)
    planes[0] = bat
    cor = planes[1]

    def prepare(k, total):
        wet = jnp.where(k < depth, sea[k], 0).astype(jnp.float32)
        fields = [ref[k] * wet for ref in (temp, salt, east, north)]
        for i in range(4):
            state[i, tile(k), :] = fields[i]
        wet_ref[tile(k), :] = wet
        dens = density(fields[0], fields[1])
        total = total + dens
        press[tile(k), :] = GRAVITY * (total - 0.5 * dens)
        return total

    total = zero
    for c in range(chunks):
        for i in range(5):
            copy_of(i, c).wait()
        total = levels_loop(c * chunk, (c + 1) * chunk, UNROLL_A, prepare, total)

    open_sides = [ok.astype(jnp.float32) for ok in (lane < 127, lane > 0, sub < 7, sub > 0)]
    base = [SIDE * ok for ok in open_sides]
    half = [0.5 * ok for ok in open_sides]

    def beside(value):
        return (pltpu.roll(value, 127, 1), pltpu.roll(value, 1, 1), pltpu.roll(value, 7, 0), pltpu.roll(value, 1, 0))

    def partial(k, carry):
        fields = [state[i, tile(k), :] for i in range(4)]
        above = [state[i, tile(k - 1), :] for i in range(4)]
        below = [state[i, tile(k + 1), :] for i in range(4)]
        wet = wet_ref[tile(k), :]
        wet_v = wet_ref[tile(k - 1), :] + wet_ref[tile(k + 1), :]
        p = press[tile(k), :]
        new = tile_update(k, fields, above, below, [beside(f) for f in fields], wet, wet_v, beside(wet),
                          p, beside(wet * p), cor, bat, base, half)
        for i in range(4):
            part[i, tile(k), :] = new[i]
        return carry

    levels_loop(0, levels, UNROLL_B, partial, 0)

    pair = lane // 2
    packed = {}
    for first, last in ((0, min(LOW, levels)), (LOW, levels)):
        columns = [zero] * 10
        for k in range(first, last):
            here = pair == k - first
            at = pl.ds(8 * (k + 1), 8)
            values = [state[i, at, :] for i in range(4)] + [wet_ref[at, :], press[at, :]]
            values = values + [part[i, at, :] for i in range(4)]
            columns = [jnp.where(here, pltpu.roll(v, 2 * (k - first) + 1, 1), c) for v, c in zip(values, columns)]
        packed[first] = columns
    even = lane % 2 == 0
    for j, (low, high) in enumerate(zip(packed[0], packed[LOW])):
        eastern = jnp.where(even, low, pltpu.roll(high, 1, 1))
        west = jnp.where(even, pltpu.roll(high, 127, 1), low)
        on[j] = jnp.where(lon_odd == 0, eastern, west)
        off[j] = jnp.where(lon_odd == 0, west, eastern)


def write_rows(levels, ref, row, state, wet_ref, part):
    rows = pl.ds(8 + row, levels, stride=8)
    planes = [state[i, rows, :] for i in range(4)] + [wet_ref[rows, :]] + [part[i, rows, :] for i in range(4)]
    for i, plane in enumerate(planes):
        ref[pl.ds(levels * i, levels), :] = plane
    left = long_of(levels) - 9 * levels
    if left:
        ref[pl.ds(9 * levels, left), :] = jnp.zeros((left, 128), jnp.float32)


def long_of(levels):
    return 8 * ((9 * levels + 7) // 8)


def rows_kernel(levels, tops, place, state, wet_ref, part, xs, fold_a):
    lat_odd = place[1] % 2
    write_rows(levels, xs, 7 - 7 * lat_odd, state, wet_ref, part)

    @pl.when(place[1] == tops)
    def _():
        rows = pl.ds(8 + 7, levels, stride=8)
        planes = [state[i, rows, :] for i in range(4)] + [wet_ref[rows, :]]
        for i, plane in enumerate(planes):
            count = min(levels, PART - levels * i)
            fold_a[pl.ds(levels * i, count), :] = plane[:count]


def sides_of(lon_odd, on_own, off_own, on, off):
    odd = lon_odd == 1
    west = [swap(jnp.where(odd, on_own[j], off_own[j])) for j in range(10)]
    east = [swap(jnp.where(odd, off_own[j], on_own[j])) for j in range(10)]
    far_west = [jnp.where(odd, on[j], off[j]) for j in range(10)]
    far_east = [jnp.where(odd, off[j], on[j]) for j in range(10)]
    return west, east, far_west, far_east


def corner_kernel(levels, tops, place, on_own, off_own, on, off, state, wet_ref, part, xs_own, zb, fold_b, corner_xs, extra):
    lon_odd = place[0] % 2
    lat_odd = place[1] % 2
    write_rows(levels, zb, 7 * lat_odd, state, wet_ref, part)
    west, east, far_west, far_east = sides_of(lon_odd, on_own, off_own, on, off)
    adds_w = side_adds(west[:6], far_west[:6], "west")
    adds_e = side_adds(east[:6], far_east[:6], "east")
    entries = far_west[:6] + adds_w + far_east[:6] + adds_e
    for ref, start, flag in ((corner_xs, 0, lat_odd == 0), (zb, long_of(levels), lat_odd == 1)):
        for r, entry in enumerate(entries):
            ref[pl.ds(start + r, 1), :] = jnp.where(flag, entry[7:8, :], entry[0:1, :])
        ref[pl.ds(start + 20, 4), :] = jnp.zeros((4, 128), jnp.float32)
    low, high = merged(adds_w, adds_e)
    for i in range(4):
        extra[i] = low[i]
        extra[4 + i] = high[i]

    @pl.when(place[1] == tops)
    def _():
        fold_b[...] = zb[pl.ds(PART, zb.shape[0] - PART), :]


def second_kernel(levels, place, part, extra, full):
    _, lane = iotas()
    ends = (lane == 0) | (lane == 127)

    def add(extra, high, k, carry):
        for i in range(4):
            more = jnp.where(ends, pltpu.roll(extra[i], turn_of(k, high), 1), 0.0)
            full[i, tile(k), :] = part[i, tile(k), :] + more
        return carry

    levels_loop(0, min(LOW, levels), UNROLL_C, functools.partial(add, [extra[i] for i in range(4)], False), 0)
    if levels > LOW:
        levels_loop(LOW, levels, UNROLL_C, functools.partial(add, [extra[4 + i] for i in range(4)], True), 0)
    zero = jnp.zeros((8, 128), jnp.float32)
    for i in range(4):
        for edge in (-1, levels):
            full[i, pl.ds(8 * (edge + 1), 8), :] = zero


def choose_kernel(levels, count, place, zb, corner_xs, *refs):
    corners = refs[count]
    odd = place[1] % 2 == 1
    at_end = pl.ds(long_of(levels), 24)
    corners[pl.ds(0, 24), :] = jnp.where(odd, corner_xs[...], zb[at_end, :])
    corners[pl.ds(24, 24), :] = jnp.where(odd, zb[at_end, :], corner_xs[...])


def third_kernel(levels, tops, place, full_in, wet_ref, columns_in, xs_own, zb_own, xs, zb, fold_a, fold_b,
                 on_own, off_own, on, off, corners,
                 temp_hbm, salt_hbm, east_hbm, north_hbm, full, halo, flipped, turned, outs, sems):
    lon_odd = place[0] % 2
    lat_odd = place[1] % 2
    odd = lat_odd == 1
    top = place[1] == tops
    sub, lane = iotas()
    bat, cor = columns_in[0], columns_in[1]
    full[...] = full_in[...]

    south_c = corners[pl.ds(0, 24), :]
    north_c = jnp.where(top, fold_b[pl.ds(long_of(levels) - PART, 24), :], corners[pl.ds(24, 24), :])
    r = lax.broadcasted_iota(jnp.int32, (24, 128), 0)
    swapped = swap(jnp.concatenate([north_c[10:20], north_c[0:10], north_c[20:24]], axis=0))
    s = r % 10
    swapped = jnp.where((s == 2) | (s == 3) | (s == 8) | (s == 9), -swapped, swapped)
    north_c = jnp.where(top, swapped, north_c)

    west, east, far_west, far_east = sides_of(lon_odd, on_own, off_own, on, off)
    far_cols = []
    for own, far, toward, base, order in ((west, far_west, "east", 0, 0), (east, far_east, "west", 10, 1)):
        new = list(far[6:10])
        south_cell = [south_c[base + i : base + i + 1, :] for i in range(6)]
        north_cell = [north_c[base + i : base + i + 1, :] for i in range(6)]
        for i, a in enumerate(side_adds(far[:6], own[:6], toward)):
            new[i] = new[i] + a
        for i, a in enumerate(side_adds(far[:6], south_cell, "south")):
            new[i] = new[i] + jnp.where(sub == 0, a, 0.0)
        for i, a in enumerate(side_adds(far[:6], north_cell, "north")):
            new[i] = new[i] + jnp.where(sub == 7, a, 0.0)
        p = GRAVITY * jnp.dot(density(new[0], new[1]), running(order), precision=HIGH,
                              preferred_element_type=jnp.float32)
        far_cols.append(new + [far[4] * p, far[4]])

    @pl.when(jnp.logical_not(top))
    def _():
        flipped[...] = jnp.where(odd, zb[pl.ds(0, long_of(levels)), :], xs[...])

    @pl.when(top)
    def _():
        mirror = 127 - lane
        for t in range(flipped.shape[0] // 8):
            at = 8 * t
            rows = fold_a[pl.ds(at, 8), :] if at < PART else fold_b[pl.ds(at - PART, 8), :]
            flipped[pl.ds(at, 8), :] = jnp.take_along_axis(rows, mirror, axis=1, mode="promise_in_bounds")

    def plane(ref, i):
        return ref[pl.ds(levels * i, levels), :]

    sign = jnp.where(top, -1.0, 1.0)
    signs = [1.0, 1.0, sign, sign, 1.0, 1.0, 1.0, sign, sign]
    north_far = [plane(flipped, i) * signs[i] for i in range(9)]
    south_far = [jnp.where(odd, plane(xs, i), plane(zb, i)) for i in range(9)]
    north_own = [jnp.where(odd, plane(zb_own, i), plane(xs_own, i)) for i in range(5)]
    south_own = [jnp.where(odd, plane(xs_own, i), plane(zb_own, i)) for i in range(5)]
    row, col = iotas((levels, levels))
    lower = jnp.where(col < row, 1.0, jnp.where(row == col, 0.5, 0.0))

    def pressures(planes):
        dens = jnp.concatenate([density(f[0], f[1]) for f in planes], axis=1)
        p = GRAVITY * jnp.dot(lower, dens, precision=HIGH, preferred_element_type=jnp.float32)
        return [p[:, 128 * j : 128 * j + 128] for j in range(len(planes))]

    before = pressures([south_far, north_far, south_own, north_own])
    lanes = lax.broadcasted_iota(jnp.int32, (levels, 128), 1)
    turned[...] = jnp.concatenate([south_c, north_c, jnp.zeros((80, 128), jnp.float32)], axis=0).T

    def in_order(odd_first):
        low = min(LOW, levels)
        parts = [turned[pl.ds(odd_first, low, stride=2), :]]
        if levels > LOW:
            parts.append(turned[pl.ds(1 - odd_first, levels - LOW, stride=2), :])
        return jnp.concatenate(parts, axis=0)

    west_c, east_c = in_order(0), in_order(1)
    results = []
    for n, (far, own, own_side, far_side, own_row) in enumerate(
        ((south_far, south_own, "south", "north", 0), (north_far, north_own, "north", "south", 7))
    ):
        far_cell = far[:5] + [before[n]]
        own_cell = own[:5] + [before[2 + n]]
        rows = pl.ds(8 + own_row, levels, stride=8)
        for i, a in enumerate(side_adds(own_cell, far_cell, own_side)):
            full[i, rows, :] = full[i, rows, :] + a
        new = []
        for i, a in enumerate(side_adds(far_cell, own_cell, far_side)):
            c = 24 * n + 6 + i
            extra = jnp.where(lanes == 0, west_c[:, c : c + 1], 0.0)
            extra = jnp.where(lanes == 127, east_c[:, c + 10 : c + 11], extra)
            new.append(far[5 + i] + a + extra)
        results.append(new)
    later = pressures(results)
    for n, (new, far) in enumerate(zip(results, (south_far, north_far))):
        for i, value in enumerate(new + [far[4] * later[n], far[4]]):
            halo[n, i, pl.ds(0, levels), :] = value

    chunk = 25 if levels % 25 == 0 else levels

    def copy_of(i, c):
        rows = pl.ds(c * chunk, chunk)
        target = (temp_hbm, salt_hbm, east_hbm, north_hbm)[i]
        return pltpu.make_async_copy(outs.at[i, rows], target.at[rows], sems.at[i, c])

    def beside(value, k, j, extra, high):
        far = pltpu.roll(extra[j], turn_of(k, high), 1)
        return (
            jnp.where(lane == 127, far, pltpu.roll(value, 127, 1)),
            jnp.where(lane == 0, far, pltpu.roll(value, 1, 1)),
            jnp.where(sub == 7, halo[1, j, pl.ds(k, 1), :], pltpu.roll(value, 7, 0)),
            jnp.where(sub == 0, halo[0, j, pl.ds(k, 1), :], pltpu.roll(value, 1, 0)),
        )

    base = [SIDE] * 4
    half = [0.5] * 4

    def last_step(extra, high, k, total):
        fields = [full[i, tile(k), :] for i in range(4)]
        above = [full[i, tile(k - 1), :] for i in range(4)]
        below = [full[i, tile(k + 1), :] for i in range(4)]
        wet = wet_ref[tile(k), :]
        wet_v = wet_ref[tile(k - 1), :] + wet_ref[tile(k + 1), :]
        dens = density(fields[0], fields[1])
        total = total + dens
        p = GRAVITY * (total - 0.5 * dens)
        new = tile_update(k, fields, above, below, [beside(f, k, i, extra, high) for i, f in enumerate(fields)],
                          wet, wet_v, beside(wet, k, 5, extra, high), p, beside(wet * p, k, 4, extra, high),
                          cor, bat, base, half)
        for i in range(4):
            outs[i, k] = new[i]
        return total

    extras = merged(far_cols[0], far_cols[1])
    total = jnp.zeros((8, 128), jnp.float32)
    for c in range(levels // chunk):
        first, last = c * chunk, (c + 1) * chunk
        for start, stop, high in ((first, min(last, LOW), False), (max(first, LOW), last, True)):
            if start < stop:
                total = levels_loop(start, stop, UNROLL_D, functools.partial(last_step, extras[int(high)], high), total)
        for i in range(4):
            copy_of(i, c).start()
    for c in range(levels // chunk):
        for i in range(4):
            copy_of(i, c).wait()


def shape(*dims):
    return jax.ShapeDtypeStruct(dims, jnp.float32)


def call(kernel, outs, ins, scratch=(), far_ins=(), far_outs=False, work=10**11):
    vmem = pl.BlockSpec(memory_space=pltpu.VMEM)
    hbm = pl.BlockSpec(memory_space=pltpu.HBM)
    anywhere = pl.BlockSpec(memory_space=pl.ANY)
    return pl.pallas_call(
        kernel,
        out_shape=outs,
        in_specs=[pl.BlockSpec(memory_space=pltpu.SMEM)] + [anywhere if i in far_ins else vmem for i in range(1, len(ins))],
        out_specs=[hbm if far_outs else vmem] * len(outs),
        scratch_shapes=list(scratch),
        compiler_params=pltpu.CompilerParams(vmem_limit_bytes=20 * 2**20),
        cost_estimate=pl.CostEstimate(flops=work, bytes_accessed=1000, transcendentals=0),
    )(*ins)


def pairs_of(names, count_lon, count_lat):
    def at(lon, lat):
        return lon * count_lat + lat if names[0] == "lon" else lat * count_lon + lon

    every = [(lon, lat) for lon in range(count_lon) for lat in range(count_lat)]
    on = [(at(o, a), at(o ^ 1, a)) for o, a in every]
    off = [(at(o, a), at((o + 1 if o % 2 else o - 1) % count_lon, a)) for o, a in every]
    xs = [(at(o, a), at(o, a ^ 1)) for o, a in every]
    zb = [(at(o, a), at(o, a + 1 if a % 2 else a - 1)) for o, a in every if 0 < a < count_lat - 1]
    top = count_lat - 1
    to_relay = [(at(o, top), at(count_lon - 1 - o, top - 1)) for o in range(count_lon)]
    from_relay = [(at(o, top - 1), at(o, top)) for o in range(count_lon)]
    return on, off, xs, zb, to_relay, from_relay


def per_device(names, count_lon, count_lat, temp, salt, east, north, sea, bathymetry, vorticity):
    levels = temp.shape[0]
    on_pairs, off_pairs, xs_pairs, zb_pairs, to_relay, from_relay = pairs_of(names, count_lon, count_lat)
    place = jnp.stack([lax.axis_index("lon"), lax.axis_index("lat")]).astype(jnp.int32)
    tall = 8 * (levels + 2)
    ten = shape(10, 8, 128)
    long = long_of(levels)
    message = shape(long, 128)
    cube = (levels, 8, 128)
    chunks = 3 if levels % 25 == 0 else 1
    raw = [pltpu.with_memory_space_constraint(x, pltpu.HBM) for x in (temp, salt, east, north, sea, bathymetry, vorticity)]
    part, wet, on_own, off_own, state, columns = call(
        functools.partial(first_kernel, levels),
        [shape(4, tall, 128), shape(tall, 128), ten, ten, shape(4, tall, 128), shape(2, 8, 128)],
        [place, *raw],
        [pltpu.VMEM((tall, 128), jnp.float32)] + [pltpu.VMEM(cube, jnp.float32)] * 4
        + [pltpu.VMEM(cube, jnp.int32), pltpu.VMEM((8, 128), jnp.int32), pltpu.SemaphoreType.DMA((5, chunks)),
           pltpu.SemaphoreType.DMA((2,))],
        far_ins=(1, 2, 3, 4, 5, 6, 7),
    )
    move = functools.partial(lax.ppermute, axis_name=names)
    on = move(on_own, perm=on_pairs)
    off = move(off_own, perm=off_pairs)
    xs_own, fold_a = call(
        functools.partial(rows_kernel, levels, count_lat - 1),
        [message, shape(PART, 128)],
        [place, state, wet, part],
        work=W_ROWS,
    )
    fold_a = move(fold_a, perm=to_relay)
    xs = move(xs_own, perm=xs_pairs)
    zb_own, fold_b, corner_xs, extra = call(
        functools.partial(corner_kernel, levels, count_lat - 1),
        [shape(long + 24, 128), shape(long + 24 - PART, 128), shape(24, 128), shape(8, 8, 128)],
        [place, on_own, off_own, on, off, state, wet, part, xs_own],
        work=W_CORNER,
    )
    fold_b = move(fold_b, perm=to_relay)
    zb = move(zb_own, perm=zb_pairs)
    corner_xs = move(corner_xs, perm=xs_pairs)
    fold_a = move(fold_a, perm=from_relay)
    fold_b = move(fold_b, perm=from_relay)
    full, = call(functools.partial(second_kernel, levels), [shape(4, tall, 128)], [place, part, extra], work=W_ADD)
    corners, = call(
        functools.partial(choose_kernel, levels, 2),
        [shape(48, 128)],
        [place, zb, corner_xs, xs, fold_a],
        far_ins=(3, 4),
        work=W_CHOOSE,
    )
    out = shape(levels, 8, 128)
    return tuple(
        call(
            functools.partial(third_kernel, levels, count_lat - 1),
            [out] * 4,
            [place, full, wet, columns, xs_own, zb_own, xs, zb, fold_a, fold_b, on_own, off_own, on, off,
             corners],
            [
                pltpu.VMEM((4, tall, 128), jnp.float32),
                pltpu.VMEM((2, 6, 8 * ((levels + 7) // 8), 128), jnp.float32),
                pltpu.VMEM((long, 128), jnp.float32),
                pltpu.VMEM((128, 128), jnp.float32),
                pltpu.VMEM((4,) + cube, jnp.float32),
                pltpu.SemaphoreType.DMA((4, chunks)),
            ],
            far_outs=True,
        )
    )


def solution(mesh):
    cube, plane = P(None, "lat", "lon"), P("lat", "lon")
    names = tuple(n for n in mesh.axis_names if n in ("lon", "lat"))
    return jax.shard_map(
        functools.partial(per_device, names, mesh.shape["lon"], mesh.shape["lat"]),
        mesh=mesh,
        in_specs=(cube,) * 5 + (plane,) * 2,
        out_specs=(cube,) * 4,
        check_vma=False,
    )
```

```python
import functools

import jax
import jax.numpy as jnp
from jax import lax
from jax.experimental import pallas as pl
from jax.experimental.pallas import tpu as pltpu
from jax.sharding import PartitionSpec as P

SIDE = 0.4
STEP = 0.1
THERMAL = 0.2
HALINE = 0.8
GRAVITY = 0.1
DRAG = 2.0
HIGH = lax.Precision.HIGHEST
LOW = 64
UNROLL_A = 25
UNROLL_B = 25
UNROLL_C = 16
UNROLL_D = 25
PART = 344
W_ROWS = 2*10**10
W_CORNER = 2*10**10
W_ADD = 2*10**10
W_CHOOSE = 2*10**10


def levels_loop(first, last, unroll, body, carry):
    count = (last - first) // unroll

    def group(index, carry):
        for step in range(unroll):
            carry = body(first + index * unroll + step, carry)
        return carry

    carry = lax.fori_loop(0, count, group, carry)
    for k in range(first + count * unroll, last):
        carry = body(k, carry)
    return carry


def tile(k):
    return pl.ds(pl.multiple_of(8 * (k + 1), 8), 8)


def density(temp, salt):
    return HALINE * salt - THERMAL * temp


def tile_update(k, fields, above, below, around, wet, wet_v, wet_around, press, press_around, cor, bat, base, half):
    signs = (-1.0, 1.0, -1.0, 1.0)
    speeds = (fields[2], fields[2], fields[3], fields[3])
    ways = [b + v * h if s > 0 else b - v * h for b, h, v, s in zip(base, half, speeds, signs)]
    own = SIDE * wet_v
    for way, wet_n in zip(ways, wet_around):
        own = own + way * wet_n
    tend = []
    for f, up, down, sides in zip(fields, above, below, around):
        t = SIDE * (up + down) - own * f
        for way, q in zip(ways, sides):
            t = t + way * q
        tend.append(t)
    slopes = [h * (m - press * w) for h, m, w in zip(half, press_around, wet_around)]
    rate = jnp.where(bat == lax.convert_element_type(k + 1, jnp.float32), DRAG, 0.0)
    tend[2] = tend[2] + (cor * fields[3] - (slopes[0] - slopes[1]) - rate * fields[2])
    tend[3] = tend[3] - (cor * fields[2] + (slopes[2] - slopes[3]) + rate * fields[3])
    scale = STEP * wet
    return [f + scale * t for f, t in zip(fields, tend)]


def from_side(centre, other, way, to_u, to_v):
    scale = STEP * centre[4]
    wet_n = other[4]
    adds = [scale * (way * (other[i] - wet_n * centre[i])) for i in range(4)]
    push = (0.5 * scale) * (wet_n * (other[5] - centre[5]))
    if to_u:
        adds[2] = adds[2] + to_u * push
    if to_v:
        adds[3] = adds[3] + to_v * push
    return adds


def way_of(cell, side):
    if side == "east":
        return SIDE - 0.5 * cell[2]
    if side == "west":
        return SIDE + 0.5 * cell[2]
    if side == "north":
        return SIDE - 0.5 * cell[3]
    return SIDE + 0.5 * cell[3]


PUSH = {"east": (-1.0, 0.0), "west": (1.0, 0.0), "north": (0.0, -1.0), "south": (0.0, 1.0)}


def side_adds(cell, other, side):
    return from_side(cell, other, way_of(cell, side), *PUSH[side])


def iotas(shape=(8, 128)):
    return lax.broadcasted_iota(jnp.int32, shape, 0), lax.broadcasted_iota(jnp.int32, shape, 1)


def swap(value):
    _, lane = iotas(value.shape)
    return jnp.where(lane % 2 == 0, pltpu.roll(value, 127, 1), pltpu.roll(value, 1, 1))


def level_of(lane, odd):
    return jnp.where(lane % 2 == odd, lane // 2, LOW + lane // 2)


def running(odd):
    row, col = iotas((128, 128))
    row, col = level_of(row, odd), level_of(col, odd)
    return jnp.where(row < col, 1.0, jnp.where(row == col, 0.5, 0.0))


def merged(west, east):
    _, lane = iotas()
    even = lane % 2 == 0
    return (
        [jnp.where(even, w, pltpu.roll(e, 126, 1)) for w, e in zip(west, east)],
        [jnp.where(even, e, w) for w, e in zip(west, east)],
    )


def turn_of(k, high):
    return (127 - 2 * (k - LOW)) if high else (128 - 2 * k)


def first_kernel(levels, place, temp_hbm, salt_hbm, east_hbm, north_hbm, sea_hbm, bat_hbm, cor_hbm,
                 part, wet_ref, on, off, state, planes, press, temp, salt, east, north, sea, bat_ref, sems, plane_sems):
    chunk = 25 if levels % 25 == 0 else levels
    chunks = levels // chunk
    inputs = ((temp_hbm, temp), (salt_hbm, salt), (east_hbm, east), (north_hbm, north), (sea_hbm, sea))

    def copy_of(i, c):
        source, target = inputs[i]
        rows = pl.ds(c * chunk, chunk)
        return pltpu.make_async_copy(source.at[rows], target.at[rows], sems.at[i, c])

    plane_copies = [
        pltpu.make_async_copy(bat_hbm, bat_ref, plane_sems.at[0]),
        pltpu.make_async_copy(cor_hbm, planes.at[1], plane_sems.at[1]),
    ]
    for copy in plane_copies:
        copy.start()
    for c in range(chunks):
        for i in range(5):
            copy_of(i, c).start()
    lon_odd = place[0] % 2
    sub, lane = iotas()
    zero = jnp.zeros((8, 128), jnp.float32)
    for i in range(4):
        for edge in (-1, levels):
            state[i, pl.ds(8 * (edge + 1), 8), :] = zero
            part[i, pl.ds(8 * (edge + 1), 8), :] = zero
    for edge in (-1, levels):
        wet_ref[pl.ds(8 * (edge + 1), 8), :] = zero
    for copy in plane_copies:
        copy.wait()
    depth = bat_ref[...]
    bat = depth.astype(jnp.float32)
    planes[0] = bat
    cor = planes[1]

    def prepare(k, total):
        wet = jnp.where(k < depth, sea[k], 0).astype(jnp.float32)
        fields = [ref[k] * wet for ref in (temp, salt, east, north)]
        for i in range(4):
            state[i, tile(k), :] = fields[i]
        wet_ref[tile(k), :] = wet
        dens = density(fields[0], fields[1])
        total = total + dens
        press[tile(k), :] = GRAVITY * (total - 0.5 * dens)
        return total

    total = zero
    for c in range(chunks):
        for i in range(5):
            copy_of(i, c).wait()
        total = levels_loop(c * chunk, (c + 1) * chunk, UNROLL_A, prepare, total)

    open_sides = [ok.astype(jnp.float32) for ok in (lane < 127, lane > 0, sub < 7, sub > 0)]
    base = [SIDE * ok for ok in open_sides]
    half = [0.5 * ok for ok in open_sides]

    def beside(value):
        return (pltpu.roll(value, 127, 1), pltpu.roll(value, 1, 1), pltpu.roll(value, 7, 0), pltpu.roll(value, 1, 0))

    def partial(k, carry):
        fields = [state[i, tile(k), :] for i in range(4)]
        above = [state[i, tile(k - 1), :] for i in range(4)]
        below = [state[i, tile(k + 1), :] for i in range(4)]
        wet = wet_ref[tile(k), :]
        wet_v = wet_ref[tile(k - 1), :] + wet_ref[tile(k + 1), :]
        p = press[tile(k), :]
        new = tile_update(k, fields, above, below, [beside(f) for f in fields], wet, wet_v, beside(wet),
                          p, beside(wet * p), cor, bat, base, half)
        for i in range(4):
            part[i, tile(k), :] = new[i]
        return carry

    levels_loop(0, levels, UNROLL_B, partial, 0)

    pair = lane // 2
    packed = {}
    for first, last in ((0, min(LOW, levels)), (LOW, levels)):
        columns = [zero] * 10
        for k in range(first, last):
            here = pair == k - first
            at = pl.ds(8 * (k + 1), 8)
            values = [state[i, at, :] for i in range(4)] + [wet_ref[at, :], press[at, :]]
            values = values + [part[i, at, :] for i in range(4)]
            columns = [jnp.where(here, pltpu.roll(v, 2 * (k - first) + 1, 1), c) for v, c in zip(values, columns)]
        packed[first] = columns
    even = lane % 2 == 0
    for j, (low, high) in enumerate(zip(packed[0], packed[LOW])):
        eastern = jnp.where(even, low, pltpu.roll(high, 1, 1))
        west = jnp.where(even, pltpu.roll(high, 127, 1), low)
        on[j] = jnp.where(lon_odd == 0, eastern, west)
        off[j] = jnp.where(lon_odd == 0, west, eastern)


def write_rows(levels, ref, row, state, wet_ref, part):
    rows = pl.ds(8 + row, levels, stride=8)
    planes = [state[i, rows, :] for i in range(4)] + [wet_ref[rows, :]] + [part[i, rows, :] for i in range(4)]
    for i, plane in enumerate(planes):
        ref[pl.ds(levels * i, levels), :] = plane
    left = long_of(levels) - 9 * levels
    if left:
        ref[pl.ds(9 * levels, left), :] = jnp.zeros((left, 128), jnp.float32)


def long_of(levels):
    return 8 * ((9 * levels + 7) // 8)


def rows_kernel(levels, tops, place, state, wet_ref, part, xs, fold_a):
    lat_odd = place[1] % 2
    write_rows(levels, xs, 7 - 7 * lat_odd, state, wet_ref, part)

    @pl.when(place[1] == tops)
    def _():
        rows = pl.ds(8 + 7, levels, stride=8)
        planes = [state[i, rows, :] for i in range(4)] + [wet_ref[rows, :]]
        for i, plane in enumerate(planes):
            count = min(levels, PART - levels * i)
            fold_a[pl.ds(levels * i, count), :] = plane[:count]


def sides_of(lon_odd, on_own, off_own, on, off):
    odd = lon_odd == 1
    west = [swap(jnp.where(odd, on_own[j], off_own[j])) for j in range(10)]
    east = [swap(jnp.where(odd, off_own[j], on_own[j])) for j in range(10)]
    far_west = [jnp.where(odd, on[j], off[j]) for j in range(10)]
    far_east = [jnp.where(odd, off[j], on[j]) for j in range(10)]
    return west, east, far_west, far_east


def corner_kernel(levels, tops, place, on_own, off_own, on, off, state, wet_ref, part, xs_own, zb, fold_b, corner_xs, extra):
    lon_odd = place[0] % 2
    lat_odd = place[1] % 2
    write_rows(levels, zb, 7 * lat_odd, state, wet_ref, part)
    west, east, far_west, far_east = sides_of(lon_odd, on_own, off_own, on, off)
    adds_w = side_adds(west[:6], far_west[:6], "west")
    adds_e = side_adds(east[:6], far_east[:6], "east")
    entries = far_west[:6] + adds_w + far_east[:6] + adds_e
    for ref, start, flag in ((corner_xs, 0, lat_odd == 0), (zb, long_of(levels), lat_odd == 1)):
        for r, entry in enumerate(entries):
            ref[pl.ds(start + r, 1), :] = jnp.where(flag, entry[7:8, :], entry[0:1, :])
        ref[pl.ds(start + 20, 4), :] = jnp.zeros((4, 128), jnp.float32)
    low, high = merged(adds_w, adds_e)
    for i in range(4):
        extra[i] = low[i]
        extra[4 + i] = high[i]

    @pl.when(place[1] == tops)
    def _():
        fold_b[...] = zb[pl.ds(PART, zb.shape[0] - PART), :]


def second_kernel(levels, place, part, extra, full):
    _, lane = iotas()
    ends = (lane == 0) | (lane == 127)

    def add(extra, high, k, carry):
        for i in range(4):
            more = jnp.where(ends, pltpu.roll(extra[i], turn_of(k, high), 1), 0.0)
            full[i, tile(k), :] = part[i, tile(k), :] + more
        return carry

    levels_loop(0, min(LOW, levels), UNROLL_C, functools.partial(add, [extra[i] for i in range(4)], False), 0)
    if levels > LOW:
        levels_loop(LOW, levels, UNROLL_C, functools.partial(add, [extra[4 + i] for i in range(4)], True), 0)
    zero = jnp.zeros((8, 128), jnp.float32)
    for i in range(4):
        for edge in (-1, levels):
            full[i, pl.ds(8 * (edge + 1), 8), :] = zero


def choose_kernel(levels, count, place, zb, corner_xs, *refs):
    corners = refs[count]
    odd = place[1] % 2 == 1
    at_end = pl.ds(long_of(levels), 24)
    corners[pl.ds(0, 24), :] = jnp.where(odd, corner_xs[...], zb[at_end, :])
    corners[pl.ds(24, 24), :] = jnp.where(odd, zb[at_end, :], corner_xs[...])


def third_kernel(levels, tops, place, full_in, wet_ref, columns_in, xs_own, zb_own, xs, zb, fold_a, fold_b,
                 on_own, off_own, on, off, corners,
                 temp_hbm, salt_hbm, east_hbm, north_hbm, full, halo, flipped, turned, outs, sems):
    lon_odd = place[0] % 2
    lat_odd = place[1] % 2
    odd = lat_odd == 1
    top = place[1] == tops
    sub, lane = iotas()
    bat, cor = columns_in[0], columns_in[1]
    full[...] = full_in[...]

    south_c = corners[pl.ds(0, 24), :]
    north_c = jnp.where(top, fold_b[pl.ds(long_of(levels) - PART, 24), :], corners[pl.ds(24, 24), :])
    r = lax.broadcasted_iota(jnp.int32, (24, 128), 0)
    swapped = swap(jnp.concatenate([north_c[10:20], north_c[0:10], north_c[20:24]], axis=0))
    s = r % 10
    swapped = jnp.where((s == 2) | (s == 3) | (s == 8) | (s == 9), -swapped, swapped)
    north_c = jnp.where(top, swapped, north_c)

    west, east, far_west, far_east = sides_of(lon_odd, on_own, off_own, on, off)
    far_cols = []
    for own, far, toward, base, order in ((west, far_west, "east", 0, 0), (east, far_east, "west", 10, 1)):
        new = list(far[6:10])
        south_cell = [south_c[base + i : base + i + 1, :] for i in range(6)]
        north_cell = [north_c[base + i : base + i + 1, :] for i in range(6)]
        for i, a in enumerate(side_adds(far[:6], own[:6], toward)):
            new[i] = new[i] + a
        for i, a in enumerate(side_adds(far[:6], south_cell, "south")):
            new[i] = new[i] + jnp.where(sub == 0, a, 0.0)
        for i, a in enumerate(side_adds(far[:6], north_cell, "north")):
            new[i] = new[i] + jnp.where(sub == 7, a, 0.0)
        p = GRAVITY * jnp.dot(density(new[0], new[1]), running(order), precision=HIGH,
                              preferred_element_type=jnp.float32)
        far_cols.append(new + [far[4] * p, far[4]])

    @pl.when(jnp.logical_not(top))
    def _():
        flipped[...] = jnp.where(odd, zb[pl.ds(0, long_of(levels)), :], xs[...])

    @pl.when(top)
    def _():
        mirror = 127 - lane
        for t in range(flipped.shape[0] // 8):
            at = 8 * t
            rows = fold_a[pl.ds(at, 8), :] if at < PART else fold_b[pl.ds(at - PART, 8), :]
            flipped[pl.ds(at, 8), :] = jnp.take_along_axis(rows, mirror, axis=1, mode="promise_in_bounds")

    def plane(ref, i):
        return ref[pl.ds(levels * i, levels), :]

    sign = jnp.where(top, -1.0, 1.0)
    signs = [1.0, 1.0, sign, sign, 1.0, 1.0, 1.0, sign, sign]
    north_far = [plane(flipped, i) * signs[i] for i in range(9)]
    south_far = [jnp.where(odd, plane(xs, i), plane(zb, i)) for i in range(9)]
    north_own = [jnp.where(odd, plane(zb_own, i), plane(xs_own, i)) for i in range(5)]
    south_own = [jnp.where(odd, plane(xs_own, i), plane(zb_own, i)) for i in range(5)]
    row, col = iotas((levels, levels))
    lower = jnp.where(col < row, 1.0, jnp.where(row == col, 0.5, 0.0))

    def pressures(planes):
        dens = jnp.concatenate([density(f[0], f[1]) for f in planes], axis=1)
        p = GRAVITY * jnp.dot(lower, dens, precision=HIGH, preferred_element_type=jnp.float32)
        return [p[:, 128 * j : 128 * j + 128] for j in range(len(planes))]

    before = pressures([south_far, north_far, south_own, north_own])
    lanes = lax.broadcasted_iota(jnp.int32, (levels, 128), 1)
    turned[...] = jnp.concatenate([south_c, north_c, jnp.zeros((80, 128), jnp.float32)], axis=0).T

    def in_order(odd_first):
        low = min(LOW, levels)
        parts = [turned[pl.ds(odd_first, low, stride=2), :]]
        if levels > LOW:
            parts.append(turned[pl.ds(1 - odd_first, levels - LOW, stride=2), :])
        return jnp.concatenate(parts, axis=0)

    west_c, east_c = in_order(0), in_order(1)
    results = []
    for n, (far, own, own_side, far_side, own_row) in enumerate(
        ((south_far, south_own, "south", "north", 0), (north_far, north_own, "north", "south", 7))
    ):
        far_cell = far[:5] + [before[n]]
        own_cell = own[:5] + [before[2 + n]]
        rows = pl.ds(8 + own_row, levels, stride=8)
        for i, a in enumerate(side_adds(own_cell, far_cell, own_side)):
            full[i, rows, :] = full[i, rows, :] + a
        new = []
        for i, a in enumerate(side_adds(far_cell, own_cell, far_side)):
            c = 24 * n + 6 + i
            extra = jnp.where(lanes == 0, west_c[:, c : c + 1], 0.0)
            extra = jnp.where(lanes == 127, east_c[:, c + 10 : c + 11], extra)
            new.append(far[5 + i] + a + extra)
        results.append(new)
    later = pressures(results)
    for n, (new, far) in enumerate(zip(results, (south_far, north_far))):
        for i, value in enumerate(new + [far[4] * later[n], far[4]]):
            halo[n, i, pl.ds(0, levels), :] = value

    chunk = 25 if levels % 25 == 0 else levels

    def copy_of(i, c):
        rows = pl.ds(c * chunk, chunk)
        target = (temp_hbm, salt_hbm, east_hbm, north_hbm)[i]
        return pltpu.make_async_copy(outs.at[i, rows], target.at[rows], sems.at[i, c])

    def beside(value, k, j, extra, high):
        far = pltpu.roll(extra[j], turn_of(k, high), 1)
        return (
            jnp.where(lane == 127, far, pltpu.roll(value, 127, 1)),
            jnp.where(lane == 0, far, pltpu.roll(value, 1, 1)),
            jnp.where(sub == 7, halo[1, j, pl.ds(k, 1), :], pltpu.roll(value, 7, 0)),
            jnp.where(sub == 0, halo[0, j, pl.ds(k, 1), :], pltpu.roll(value, 1, 0)),
        )

    base = [SIDE] * 4
    half = [0.5] * 4

    def last_step(extra, high, k, total):
        fields = [full[i, tile(k), :] for i in range(4)]
        above = [full[i, tile(k - 1), :] for i in range(4)]
        below = [full[i, tile(k + 1), :] for i in range(4)]
        wet = wet_ref[tile(k), :]
        wet_v = wet_ref[tile(k - 1), :] + wet_ref[tile(k + 1), :]
        dens = density(fields[0], fields[1])
        total = total + dens
        p = GRAVITY * (total - 0.5 * dens)
        new = tile_update(k, fields, above, below, [beside(f, k, i, extra, high) for i, f in enumerate(fields)],
                          wet, wet_v, beside(wet, k, 5, extra, high), p, beside(wet * p, k, 4, extra, high),
                          cor, bat, base, half)
        for i in range(4):
            outs[i, k] = new[i]
        return total

    extras = merged(far_cols[0], far_cols[1])
    total = jnp.zeros((8, 128), jnp.float32)
    for c in range(levels // chunk):
        first, last = c * chunk, (c + 1) * chunk
        for start, stop, high in ((first, min(last, LOW), False), (max(first, LOW), last, True)):
            if start < stop:
                total = levels_loop(start, stop, UNROLL_D, functools.partial(last_step, extras[int(high)], high), total)
        for i in range(4):
            copy_of(i, c).start()
    for c in range(levels // chunk):
        for i in range(4):
            copy_of(i, c).wait()


def shape(*dims):
    return jax.ShapeDtypeStruct(dims, jnp.float32)


def call(kernel, outs, ins, scratch=(), far_ins=(), far_outs=False, work=2*10**10):
    vmem = pl.BlockSpec(memory_space=pltpu.VMEM)
    hbm = pl.BlockSpec(memory_space=pltpu.HBM)
    anywhere = pl.BlockSpec(memory_space=pl.ANY)
    return pl.pallas_call(
        kernel,
        out_shape=outs,
        in_specs=[pl.BlockSpec(memory_space=pltpu.SMEM)] + [anywhere if i in far_ins else vmem for i in range(1, len(ins))],
        out_specs=[hbm if far_outs else vmem] * len(outs),
        scratch_shapes=list(scratch),
        compiler_params=pltpu.CompilerParams(vmem_limit_bytes=20 * 2**20),
        cost_estimate=pl.CostEstimate(flops=work, bytes_accessed=1000, transcendentals=0),
    )(*ins)


def pairs_of(names, count_lon, count_lat):
    def at(lon, lat):
        return lon * count_lat + lat if names[0] == "lon" else lat * count_lon + lon

    every = [(lon, lat) for lon in range(count_lon) for lat in range(count_lat)]
    on = [(at(o, a), at(o ^ 1, a)) for o, a in every]
    off = [(at(o, a), at((o + 1 if o % 2 else o - 1) % count_lon, a)) for o, a in every]
    xs = [(at(o, a), at(o, a ^ 1)) for o, a in every]
    zb = [(at(o, a), at(o, a + 1 if a % 2 else a - 1)) for o, a in every if 0 < a < count_lat - 1]
    top = count_lat - 1
    to_relay = [(at(o, top), at(count_lon - 1 - o, top - 1)) for o in range(count_lon)]
    from_relay = [(at(o, top - 1), at(o, top)) for o in range(count_lon)]
    return on, off, xs, zb, to_relay, from_relay


def per_device(names, count_lon, count_lat, temp, salt, east, north, sea, bathymetry, vorticity):
    levels = temp.shape[0]
    on_pairs, off_pairs, xs_pairs, zb_pairs, to_relay, from_relay = pairs_of(names, count_lon, count_lat)
    place = jnp.stack([lax.axis_index("lon"), lax.axis_index("lat")]).astype(jnp.int32)
    tall = 8 * (levels + 2)
    ten = shape(10, 8, 128)
    long = long_of(levels)
    message = shape(long, 128)
    cube = (levels, 8, 128)
    chunks = 3 if levels % 25 == 0 else 1
    raw = [pltpu.with_memory_space_constraint(x, pltpu.HBM) for x in (temp, salt, east, north, sea, bathymetry, vorticity)]
    part, wet, on_own, off_own, state, columns = call(
        functools.partial(first_kernel, levels),
        [shape(4, tall, 128), shape(tall, 128), ten, ten, shape(4, tall, 128), shape(2, 8, 128)],
        [place, *raw],
        [pltpu.VMEM((tall, 128), jnp.float32)] + [pltpu.VMEM(cube, jnp.float32)] * 4
        + [pltpu.VMEM(cube, jnp.int32), pltpu.VMEM((8, 128), jnp.int32), pltpu.SemaphoreType.DMA((5, chunks)),
           pltpu.SemaphoreType.DMA((2,))],
        far_ins=(1, 2, 3, 4, 5, 6, 7),
    )
    move = functools.partial(lax.ppermute, axis_name=names)
    on = move(on_own, perm=on_pairs)
    off = move(off_own, perm=off_pairs)
    xs_own, fold_a = call(
        functools.partial(rows_kernel, levels, count_lat - 1),
        [message, shape(PART, 128)],
        [place, state, wet, part],
        work=W_ROWS,
    )
    fold_a = move(fold_a, perm=to_relay)
    xs = move(xs_own, perm=xs_pairs)
    zb_own, fold_b, corner_xs, extra = call(
        functools.partial(corner_kernel, levels, count_lat - 1),
        [shape(long + 24, 128), shape(long + 24 - PART, 128), shape(24, 128), shape(8, 8, 128)],
        [place, on_own, off_own, on, off, state, wet, part, xs_own],
        work=W_CORNER,
    )
    fold_b = move(fold_b, perm=to_relay)
    zb = move(zb_own, perm=zb_pairs)
    corner_xs = move(corner_xs, perm=xs_pairs)
    fold_a = move(fold_a, perm=from_relay)
    fold_b = move(fold_b, perm=from_relay)
    full, = call(functools.partial(second_kernel, levels), [shape(4, tall, 128)], [place, part, extra], work=W_ADD)
    corners, = call(
        functools.partial(choose_kernel, levels, 2),
        [shape(48, 128)],
        [place, zb, corner_xs, xs, fold_a],
        far_ins=(3, 4),
        work=W_CHOOSE,
    )
    out = shape(levels, 8, 128)
    return tuple(
        call(
            functools.partial(third_kernel, levels, count_lat - 1),
            [out] * 4,
            [place, full, wet, columns, xs_own, zb_own, xs, zb, fold_a, fold_b, on_own, off_own, on, off,
             corners],
            [
                pltpu.VMEM((4, tall, 128), jnp.float32),
                pltpu.VMEM((2, 6, 8 * ((levels + 7) // 8), 128), jnp.float32),
                pltpu.VMEM((long, 128), jnp.float32),
                pltpu.VMEM((128, 128), jnp.float32),
                pltpu.VMEM((4,) + cube, jnp.float32),
                pltpu.SemaphoreType.DMA((4, chunks)),
            ],
            far_outs=True,
        )
    )


def solution(mesh):
    cube, plane = P(None, "lat", "lon"), P("lat", "lon")
    names = tuple(n for n in mesh.axis_names if n in ("lon", "lat"))
    return jax.shard_map(
        functools.partial(per_device, names, mesh.shape["lon"], mesh.shape["lat"]),
        mesh=mesh,
        in_specs=(cube,) * 5 + (plane,) * 2,
        out_specs=(cube,) * 4,
        check_vma=False,
    )
```

```python
import functools

import jax
import jax.numpy as jnp
from jax import lax
from jax.experimental import pallas as pl
from jax.experimental.pallas import tpu as pltpu
from jax.sharding import PartitionSpec as P

SIDE = 0.4
STEP = 0.1
THERMAL = 0.2
HALINE = 0.8
GRAVITY = 0.1
DRAG = 2.0
HIGH = lax.Precision.HIGHEST
LOW = 64
UNROLL_A = 25
UNROLL_B = 25
UNROLL_C = 16
UNROLL_D = 25
PART = 448
W_ROWS = 2*10**10
W_CORNER = 2*10**10
W_ADD = 2*10**10
W_CHOOSE = 2*10**10


def levels_loop(first, last, unroll, body, carry):
    count = (last - first) // unroll

    def group(index, carry):
        for step in range(unroll):
            carry = body(first + index * unroll + step, carry)
        return carry

    carry = lax.fori_loop(0, count, group, carry)
    for k in range(first + count * unroll, last):
        carry = body(k, carry)
    return carry


def tile(k):
    return pl.ds(pl.multiple_of(8 * (k + 1), 8), 8)


def density(temp, salt):
    return HALINE * salt - THERMAL * temp


def tile_update(k, fields, above, below, around, wet, wet_v, wet_around, press, press_around, cor, bat, base, half):
    signs = (-1.0, 1.0, -1.0, 1.0)
    speeds = (fields[2], fields[2], fields[3], fields[3])
    ways = [b + v * h if s > 0 else b - v * h for b, h, v, s in zip(base, half, speeds, signs)]
    own = SIDE * wet_v
    for way, wet_n in zip(ways, wet_around):
        own = own + way * wet_n
    tend = []
    for f, up, down, sides in zip(fields, above, below, around):
        t = SIDE * (up + down) - own * f
        for way, q in zip(ways, sides):
            t = t + way * q
        tend.append(t)
    slopes = [h * (m - press * w) for h, m, w in zip(half, press_around, wet_around)]
    rate = jnp.where(bat == lax.convert_element_type(k + 1, jnp.float32), DRAG, 0.0)
    tend[2] = tend[2] + (cor * fields[3] - (slopes[0] - slopes[1]) - rate * fields[2])
    tend[3] = tend[3] - (cor * fields[2] + (slopes[2] - slopes[3]) + rate * fields[3])
    scale = STEP * wet
    return [f + scale * t for f, t in zip(fields, tend)]


def from_side(centre, other, way, to_u, to_v):
    scale = STEP * centre[4]
    wet_n = other[4]
    adds = [scale * (way * (other[i] - wet_n * centre[i])) for i in range(4)]
    push = (0.5 * scale) * (wet_n * (other[5] - centre[5]))
    if to_u:
        adds[2] = adds[2] + to_u * push
    if to_v:
        adds[3] = adds[3] + to_v * push
    return adds


def way_of(cell, side):
    if side == "east":
        return SIDE - 0.5 * cell[2]
    if side == "west":
        return SIDE + 0.5 * cell[2]
    if side == "north":
        return SIDE - 0.5 * cell[3]
    return SIDE + 0.5 * cell[3]


PUSH = {"east": (-1.0, 0.0), "west": (1.0, 0.0), "north": (0.0, -1.0), "south": (0.0, 1.0)}


def side_adds(cell, other, side):
    return from_side(cell, other, way_of(cell, side), *PUSH[side])


def iotas(shape=(8, 128)):
    return lax.broadcasted_iota(jnp.int32, shape, 0), lax.broadcasted_iota(jnp.int32, shape, 1)


def swap(value):
    _, lane = iotas(value.shape)
    return jnp.where(lane % 2 == 0, pltpu.roll(value, 127, 1), pltpu.roll(value, 1, 1))


def level_of(lane, odd):
    return jnp.where(lane % 2 == odd, lane // 2, LOW + lane // 2)


def running(odd):
    row, col = iotas((128, 128))
    row, col = level_of(row, odd), level_of(col, odd)
    return jnp.where(row < col, 1.0, jnp.where(row == col, 0.5, 0.0))


def merged(west, east):
    _, lane = iotas()
    even = lane % 2 == 0
    return (
        [jnp.where(even, w, pltpu.roll(e, 126, 1)) for w, e in zip(west, east)],
        [jnp.where(even, e, w) for w, e in zip(west, east)],
    )


def turn_of(k, high):
    return (127 - 2 * (k - LOW)) if high else (128 - 2 * k)


def first_kernel(levels, place, temp_hbm, salt_hbm, east_hbm, north_hbm, sea_hbm, bat_hbm, cor_hbm,
                 part, wet_ref, on, off, state, planes, press, temp, salt, east, north, sea, bat_ref, sems, plane_sems):
    chunk = 25 if levels % 25 == 0 else levels
    chunks = levels // chunk
    inputs = ((temp_hbm, temp), (salt_hbm, salt), (east_hbm, east), (north_hbm, north), (sea_hbm, sea))

    def copy_of(i, c):
        source, target = inputs[i]
        rows = pl.ds(c * chunk, chunk)
        return pltpu.make_async_copy(source.at[rows], target.at[rows], sems.at[i, c])

    plane_copies = [
        pltpu.make_async_copy(bat_hbm, bat_ref, plane_sems.at[0]),
        pltpu.make_async_copy(cor_hbm, planes.at[1], plane_sems.at[1]),
    ]
    for copy in plane_copies:
        copy.start()
    for c in range(chunks):
        for i in range(5):
            copy_of(i, c).start()
    lon_odd = place[0] % 2
    sub, lane = iotas()
    zero = jnp.zeros((8, 128), jnp.float32)
    for i in range(4):
        for edge in (-1, levels):
            state[i, pl.ds(8 * (edge + 1), 8), :] = zero
            part[i, pl.ds(8 * (edge + 1), 8), :] = zero
    for edge in (-1, levels):
        wet_ref[pl.ds(8 * (edge + 1), 8), :] = zero
    for copy in plane_copies:
        copy.wait()
    depth = bat_ref[...]
    bat = depth.astype(jnp.float32)
    planes[0] = bat
    cor = planes[1]

    def prepare(k, total):
        wet = jnp.where(k < depth, sea[k], 0).astype(jnp.float32)
        fields = [ref[k] * wet for ref in (temp, salt, east, north)]
        for i in range(4):
            state[i, tile(k), :] = fields[i]
        wet_ref[tile(k), :] = wet
        dens = density(fields[0], fields[1])
        total = total + dens
        press[tile(k), :] = GRAVITY * (total - 0.5 * dens)
        return total

    total = zero
    for c in range(chunks):
        for i in range(5):
            copy_of(i, c).wait()
        total = levels_loop(c * chunk, (c + 1) * chunk, UNROLL_A, prepare, total)

    open_sides = [ok.astype(jnp.float32) for ok in (lane < 127, lane > 0, sub < 7, sub > 0)]
    base = [SIDE * ok for ok in open_sides]
    half = [0.5 * ok for ok in open_sides]

    def beside(value):
        return (pltpu.roll(value, 127, 1), pltpu.roll(value, 1, 1), pltpu.roll(value, 7, 0), pltpu.roll(value, 1, 0))

    def partial(k, carry):
        fields = [state[i, tile(k), :] for i in range(4)]
        above = [state[i, tile(k - 1), :] for i in range(4)]
        below = [state[i, tile(k + 1), :] for i in range(4)]
        wet = wet_ref[tile(k), :]
        wet_v = wet_ref[tile(k - 1), :] + wet_ref[tile(k + 1), :]
        p = press[tile(k), :]
        new = tile_update(k, fields, above, below, [beside(f) for f in fields], wet, wet_v, beside(wet),
                          p, beside(wet * p), cor, bat, base, half)
        for i in range(4):
            part[i, tile(k), :] = new[i]
        return carry

    levels_loop(0, levels, UNROLL_B, partial, 0)

    pair = lane // 2
    packed = {}
    for first, last in ((0, min(LOW, levels)), (LOW, levels)):
        columns = [zero] * 10
        for k in range(first, last):
            here = pair == k - first
            at = pl.ds(8 * (k + 1), 8)
            values = [state[i, at, :] for i in range(4)] + [wet_ref[at, :], press[at, :]]
            values = values + [part[i, at, :] for i in range(4)]
            columns = [jnp.where(here, pltpu.roll(v, 2 * (k - first) + 1, 1), c) for v, c in zip(values, columns)]
        packed[first] = columns
    even = lane % 2 == 0
    for j, (low, high) in enumerate(zip(packed[0], packed[LOW])):
        eastern = jnp.where(even, low, pltpu.roll(high, 1, 1))
        west = jnp.where(even, pltpu.roll(high, 127, 1), low)
        on[j] = jnp.where(lon_odd == 0, eastern, west)
        off[j] = jnp.where(lon_odd == 0, west, eastern)


def write_rows(levels, ref, row, state, wet_ref, part):
    rows = pl.ds(8 + row, levels, stride=8)
    planes = [state[i, rows, :] for i in range(4)] + [wet_ref[rows, :]] + [part[i, rows, :] for i in range(4)]
    for i, plane in enumerate(planes):
        ref[pl.ds(levels * i, levels), :] = plane
    left = long_of(levels) - 9 * levels
    if left:
        ref[pl.ds(9 * levels, left), :] = jnp.zeros((left, 128), jnp.float32)


def long_of(levels):
    return 8 * ((9 * levels + 7) // 8)


def rows_kernel(levels, tops, place, state, wet_ref, part, xs, fold_a):
    lat_odd = place[1] % 2
    write_rows(levels, xs, 7 - 7 * lat_odd, state, wet_ref, part)

    @pl.when(place[1] == tops)
    def _():
        rows = pl.ds(8 + 7, levels, stride=8)
        planes = [state[i, rows, :] for i in range(4)] + [wet_ref[rows, :]] + [part[i, rows, :] for i in range(4)]
        for i, plane in enumerate(planes):
            count = min(levels, PART - levels * i)
            if count > 0:
                fold_a[pl.ds(levels * i, count), :] = plane[:count]


def sides_of(lon_odd, on_own, off_own, on, off):
    odd = lon_odd == 1
    west = [swap(jnp.where(odd, on_own[j], off_own[j])) for j in range(10)]
    east = [swap(jnp.where(odd, off_own[j], on_own[j])) for j in range(10)]
    far_west = [jnp.where(odd, on[j], off[j]) for j in range(10)]
    far_east = [jnp.where(odd, off[j], on[j]) for j in range(10)]
    return west, east, far_west, far_east


def corner_kernel(levels, tops, place, on_own, off_own, on, off, state, wet_ref, part, xs_own, zb, fold_b, corner_xs, extra):
    lon_odd = place[0] % 2
    lat_odd = place[1] % 2
    write_rows(levels, zb, 7 * lat_odd, state, wet_ref, part)
    west, east, far_west, far_east = sides_of(lon_odd, on_own, off_own, on, off)
    adds_w = side_adds(west[:6], far_west[:6], "west")
    adds_e = side_adds(east[:6], far_east[:6], "east")
    entries = far_west[:6] + adds_w + far_east[:6] + adds_e
    for ref, start, flag in ((corner_xs, 0, lat_odd == 0), (zb, long_of(levels), lat_odd == 1)):
        for r, entry in enumerate(entries):
            ref[pl.ds(start + r, 1), :] = jnp.where(flag, entry[7:8, :], entry[0:1, :])
        ref[pl.ds(start + 20, 4), :] = jnp.zeros((4, 128), jnp.float32)
    low, high = merged(adds_w, adds_e)
    for i in range(4):
        extra[i] = low[i]
        extra[4 + i] = high[i]

    @pl.when(place[1] == tops)
    def _():
        fold_b[...] = zb[pl.ds(PART, zb.shape[0] - PART), :]


def second_kernel(levels, place, part, extra, full):
    _, lane = iotas()
    ends = (lane == 0) | (lane == 127)

    def add(extra, high, k, carry):
        for i in range(4):
            more = jnp.where(ends, pltpu.roll(extra[i], turn_of(k, high), 1), 0.0)
            full[i, tile(k), :] = part[i, tile(k), :] + more
        return carry

    levels_loop(0, min(LOW, levels), UNROLL_C, functools.partial(add, [extra[i] for i in range(4)], False), 0)
    if levels > LOW:
        levels_loop(LOW, levels, UNROLL_C, functools.partial(add, [extra[4 + i] for i in range(4)], True), 0)
    zero = jnp.zeros((8, 128), jnp.float32)
    for i in range(4):
        for edge in (-1, levels):
            full[i, pl.ds(8 * (edge + 1), 8), :] = zero


def choose_kernel(levels, count, place, zb, corner_xs, *refs):
    corners = refs[count]
    odd = place[1] % 2 == 1
    at_end = pl.ds(long_of(levels), 24)
    corners[pl.ds(0, 24), :] = jnp.where(odd, corner_xs[...], zb[at_end, :])
    corners[pl.ds(24, 24), :] = jnp.where(odd, zb[at_end, :], corner_xs[...])


def third_kernel(levels, tops, place, full_in, wet_ref, columns_in, xs_own, zb_own, xs, zb, fold_a, fold_b,
                 on_own, off_own, on, off, corners,
                 temp_hbm, salt_hbm, east_hbm, north_hbm, full, halo, flipped, turned, outs, sems):
    lon_odd = place[0] % 2
    lat_odd = place[1] % 2
    odd = lat_odd == 1
    top = place[1] == tops
    sub, lane = iotas()
    bat, cor = columns_in[0], columns_in[1]
    full[...] = full_in[...]

    south_c = corners[pl.ds(0, 24), :]
    north_c = jnp.where(top, fold_b[pl.ds(long_of(levels) - PART, 24), :], corners[pl.ds(24, 24), :])
    r = lax.broadcasted_iota(jnp.int32, (24, 128), 0)
    swapped = swap(jnp.concatenate([north_c[10:20], north_c[0:10], north_c[20:24]], axis=0))
    s = r % 10
    swapped = jnp.where((s == 2) | (s == 3) | (s == 8) | (s == 9), -swapped, swapped)
    north_c = jnp.where(top, swapped, north_c)

    west, east, far_west, far_east = sides_of(lon_odd, on_own, off_own, on, off)
    far_cols = []
    for own, far, toward, base, order in ((west, far_west, "east", 0, 0), (east, far_east, "west", 10, 1)):
        new = list(far[6:10])
        south_cell = [south_c[base + i : base + i + 1, :] for i in range(6)]
        north_cell = [north_c[base + i : base + i + 1, :] for i in range(6)]
        for i, a in enumerate(side_adds(far[:6], own[:6], toward)):
            new[i] = new[i] + a
        for i, a in enumerate(side_adds(far[:6], south_cell, "south")):
            new[i] = new[i] + jnp.where(sub == 0, a, 0.0)
        for i, a in enumerate(side_adds(far[:6], north_cell, "north")):
            new[i] = new[i] + jnp.where(sub == 7, a, 0.0)
        p = GRAVITY * jnp.dot(density(new[0], new[1]), running(order), precision=HIGH,
                              preferred_element_type=jnp.float32)
        far_cols.append(new + [far[4] * p, far[4]])

    @pl.when(jnp.logical_not(top))
    def _():
        flipped[...] = jnp.where(odd, zb[pl.ds(0, long_of(levels)), :], xs[...])

    @pl.when(top)
    def _():
        mirror = 127 - lane
        for t in range(flipped.shape[0] // 8):
            at = 8 * t
            rows = fold_a[pl.ds(at, 8), :] if at < PART else fold_b[pl.ds(at - PART, 8), :]
            flipped[pl.ds(at, 8), :] = jnp.take_along_axis(rows, mirror, axis=1, mode="promise_in_bounds")

    def plane(ref, i):
        return ref[pl.ds(levels * i, levels), :]

    sign = jnp.where(top, -1.0, 1.0)
    signs = [1.0, 1.0, sign, sign, 1.0, 1.0, 1.0, sign, sign]
    north_far = [plane(flipped, i) * signs[i] for i in range(9)]
    south_far = [jnp.where(odd, plane(xs, i), plane(zb, i)) for i in range(9)]
    north_own = [jnp.where(odd, plane(zb_own, i), plane(xs_own, i)) for i in range(5)]
    south_own = [jnp.where(odd, plane(xs_own, i), plane(zb_own, i)) for i in range(5)]
    row, col = iotas((levels, levels))
    lower = jnp.where(col < row, 1.0, jnp.where(row == col, 0.5, 0.0))

    def pressures(planes):
        dens = jnp.concatenate([density(f[0], f[1]) for f in planes], axis=1)
        p = GRAVITY * jnp.dot(lower, dens, precision=HIGH, preferred_element_type=jnp.float32)
        return [p[:, 128 * j : 128 * j + 128] for j in range(len(planes))]

    before = pressures([south_far, north_far, south_own, north_own])
    lanes = lax.broadcasted_iota(jnp.int32, (levels, 128), 1)
    turned[...] = jnp.concatenate([south_c, north_c, jnp.zeros((80, 128), jnp.float32)], axis=0).T

    def in_order(odd_first):
        low = min(LOW, levels)
        parts = [turned[pl.ds(odd_first, low, stride=2), :]]
        if levels > LOW:
            parts.append(turned[pl.ds(1 - odd_first, levels - LOW, stride=2), :])
        return jnp.concatenate(parts, axis=0)

    west_c, east_c = in_order(0), in_order(1)
    results = []
    for n, (far, own, own_side, far_side, own_row) in enumerate(
        ((south_far, south_own, "south", "north", 0), (north_far, north_own, "north", "south", 7))
    ):
        far_cell = far[:5] + [before[n]]
        own_cell = own[:5] + [before[2 + n]]
        rows = pl.ds(8 + own_row, levels, stride=8)
        for i, a in enumerate(side_adds(own_cell, far_cell, own_side)):
            full[i, rows, :] = full[i, rows, :] + a
        new = []
        for i, a in enumerate(side_adds(far_cell, own_cell, far_side)):
            c = 24 * n + 6 + i
            extra = jnp.where(lanes == 0, west_c[:, c : c + 1], 0.0)
            extra = jnp.where(lanes == 127, east_c[:, c + 10 : c + 11], extra)
            new.append(far[5 + i] + a + extra)
        results.append(new)
    later = pressures(results)
    for n, (new, far) in enumerate(zip(results, (south_far, north_far))):
        for i, value in enumerate(new + [far[4] * later[n], far[4]]):
            halo[n, i, pl.ds(0, levels), :] = value

    chunk = 25 if levels % 25 == 0 else levels

    def copy_of(i, c):
        rows = pl.ds(c * chunk, chunk)
        target = (temp_hbm, salt_hbm, east_hbm, north_hbm)[i]
        return pltpu.make_async_copy(outs.at[i, rows], target.at[rows], sems.at[i, c])

    def beside(value, k, j, extra, high):
        far = pltpu.roll(extra[j], turn_of(k, high), 1)
        return (
            jnp.where(lane == 127, far, pltpu.roll(value, 127, 1)),
            jnp.where(lane == 0, far, pltpu.roll(value, 1, 1)),
            jnp.where(sub == 7, halo[1, j, pl.ds(k, 1), :], pltpu.roll(value, 7, 0)),
            jnp.where(sub == 0, halo[0, j, pl.ds(k, 1), :], pltpu.roll(value, 1, 0)),
        )

    base = [SIDE] * 4
    half = [0.5] * 4

    def last_step(extra, high, k, total):
        fields = [full[i, tile(k), :] for i in range(4)]
        above = [full[i, tile(k - 1), :] for i in range(4)]
        below = [full[i, tile(k + 1), :] for i in range(4)]
        wet = wet_ref[tile(k), :]
        wet_v = wet_ref[tile(k - 1), :] + wet_ref[tile(k + 1), :]
        dens = density(fields[0], fields[1])
        total = total + dens
        p = GRAVITY * (total - 0.5 * dens)
        new = tile_update(k, fields, above, below, [beside(f, k, i, extra, high) for i, f in enumerate(fields)],
                          wet, wet_v, beside(wet, k, 5, extra, high), p, beside(wet * p, k, 4, extra, high),
                          cor, bat, base, half)
        for i in range(4):
            outs[i, k] = new[i]
        return total

    extras = merged(far_cols[0], far_cols[1])
    total = jnp.zeros((8, 128), jnp.float32)
    for c in range(levels // chunk):
        first, last = c * chunk, (c + 1) * chunk
        for start, stop, high in ((first, min(last, LOW), False), (max(first, LOW), last, True)):
            if start < stop:
                total = levels_loop(start, stop, UNROLL_D, functools.partial(last_step, extras[int(high)], high), total)
        for i in range(4):
            copy_of(i, c).start()
    for c in range(levels // chunk):
        for i in range(4):
            copy_of(i, c).wait()


def shape(*dims):
    return jax.ShapeDtypeStruct(dims, jnp.float32)


def call(kernel, outs, ins, scratch=(), far_ins=(), far_outs=False, work=2*10**10):
    vmem = pl.BlockSpec(memory_space=pltpu.VMEM)
    hbm = pl.BlockSpec(memory_space=pltpu.HBM)
    anywhere = pl.BlockSpec(memory_space=pl.ANY)
    return pl.pallas_call(
        kernel,
        out_shape=outs,
        in_specs=[pl.BlockSpec(memory_space=pltpu.SMEM)] + [anywhere if i in far_ins else vmem for i in range(1, len(ins))],
        out_specs=[hbm if far_outs else vmem] * len(outs),
        scratch_shapes=list(scratch),
        compiler_params=pltpu.CompilerParams(vmem_limit_bytes=20 * 2**20),
        cost_estimate=pl.CostEstimate(flops=work, bytes_accessed=1000, transcendentals=0),
    )(*ins)


def pairs_of(names, count_lon, count_lat):
    def at(lon, lat):
        return lon * count_lat + lat if names[0] == "lon" else lat * count_lon + lon

    every = [(lon, lat) for lon in range(count_lon) for lat in range(count_lat)]
    on = [(at(o, a), at(o ^ 1, a)) for o, a in every]
    off = [(at(o, a), at((o + 1 if o % 2 else o - 1) % count_lon, a)) for o, a in every]
    xs = [(at(o, a), at(o, a ^ 1)) for o, a in every]
    zb = [(at(o, a), at(o, a + 1 if a % 2 else a - 1)) for o, a in every if 0 < a < count_lat - 1]
    top = count_lat - 1
    to_relay = [(at(o, top), at(count_lon - 1 - o, top - 1)) for o in range(count_lon)]
    from_relay = [(at(o, top - 1), at(o, top)) for o in range(count_lon)]
    return on, off, xs, zb, to_relay, from_relay


def per_device(names, count_lon, count_lat, temp, salt, east, north, sea, bathymetry, vorticity):
    levels = temp.shape[0]
    on_pairs, off_pairs, xs_pairs, zb_pairs, to_relay, from_relay = pairs_of(names, count_lon, count_lat)
    place = jnp.stack([lax.axis_index("lon"), lax.axis_index("lat")]).astype(jnp.int32)
    tall = 8 * (levels + 2)
    ten = shape(10, 8, 128)
    long = long_of(levels)
    message = shape(long, 128)
    cube = (levels, 8, 128)
    chunks = 3 if levels % 25 == 0 else 1
    raw = [pltpu.with_memory_space_constraint(x, pltpu.HBM) for x in (temp, salt, east, north, sea, bathymetry, vorticity)]
    part, wet, on_own, off_own, state, columns = call(
        functools.partial(first_kernel, levels),
        [shape(4, tall, 128), shape(tall, 128), ten, ten, shape(4, tall, 128), shape(2, 8, 128)],
        [place, *raw],
        [pltpu.VMEM((tall, 128), jnp.float32)] + [pltpu.VMEM(cube, jnp.float32)] * 4
        + [pltpu.VMEM(cube, jnp.int32), pltpu.VMEM((8, 128), jnp.int32), pltpu.SemaphoreType.DMA((5, chunks)),
           pltpu.SemaphoreType.DMA((2,))],
        far_ins=(1, 2, 3, 4, 5, 6, 7),
    )
    move = functools.partial(lax.ppermute, axis_name=names)
    on = move(on_own, perm=on_pairs)
    off = move(off_own, perm=off_pairs)
    xs_own, fold_a = call(
        functools.partial(rows_kernel, levels, count_lat - 1),
        [message, shape(PART, 128)],
        [place, state, wet, part],
        work=W_ROWS,
    )
    fold_a = move(fold_a, perm=to_relay)
    xs = move(xs_own, perm=xs_pairs)
    zb_own, fold_b, corner_xs, extra = call(
        functools.partial(corner_kernel, levels, count_lat - 1),
        [shape(long + 24, 128), shape(long + 24 - PART, 128), shape(24, 128), shape(8, 8, 128)],
        [place, on_own, off_own, on, off, state, wet, part, xs_own],
        work=W_CORNER,
    )
    fold_b = move(fold_b, perm=to_relay)
    zb = move(zb_own, perm=zb_pairs)
    corner_xs = move(corner_xs, perm=xs_pairs)
    fold_a = move(fold_a, perm=from_relay)
    fold_b = move(fold_b, perm=from_relay)
    full, = call(functools.partial(second_kernel, levels), [shape(4, tall, 128)], [place, part, extra], work=W_ADD)
    corners, = call(
        functools.partial(choose_kernel, levels, 2),
        [shape(48, 128)],
        [place, zb, corner_xs, xs, fold_a],
        far_ins=(3, 4),
        work=W_CHOOSE,
    )
    out = shape(levels, 8, 128)
    return tuple(
        call(
            functools.partial(third_kernel, levels, count_lat - 1),
            [out] * 4,
            [place, full, wet, columns, xs_own, zb_own, xs, zb, fold_a, fold_b, on_own, off_own, on, off,
             corners],
            [
                pltpu.VMEM((4, tall, 128), jnp.float32),
                pltpu.VMEM((2, 6, 8 * ((levels + 7) // 8), 128), jnp.float32),
                pltpu.VMEM((long, 128), jnp.float32),
                pltpu.VMEM((128, 128), jnp.float32),
                pltpu.VMEM((4,) + cube, jnp.float32),
                pltpu.SemaphoreType.DMA((4, chunks)),
            ],
            far_outs=True,
        )
    )


def solution(mesh):
    cube, plane = P(None, "lat", "lon"), P("lat", "lon")
    names = tuple(n for n in mesh.axis_names if n in ("lon", "lat"))
    return jax.shard_map(
        functools.partial(per_device, names, mesh.shape["lon"], mesh.shape["lat"]),
        mesh=mesh,
        in_specs=(cube,) * 5 + (plane,) * 2,
        out_specs=(cube,) * 4,
        check_vma=False,
    )
```

```python
import functools

import jax
import jax.numpy as jnp
from jax import lax
from jax.experimental import pallas as pl
from jax.experimental.pallas import tpu as pltpu
from jax.sharding import PartitionSpec as P

SIDE = 0.4
STEP = 0.1
THERMAL = 0.2
HALINE = 0.8
GRAVITY = 0.1
DRAG = 2.0
HIGH = lax.Precision.HIGHEST
LOW = 64
UNROLL_A = 25
UNROLL_B = 25
UNROLL_C = 16
UNROLL_D = 25
PART = 448
W_ROWS = 2*10**10
W_CORNER = 2*10**10
W_ADD = 2*10**10
W_CHOOSE = 2*10**10


def levels_loop(first, last, unroll, body, carry):
    count = (last - first) // unroll

    def group(index, carry):
        for step in range(unroll):
            carry = body(first + index * unroll + step, carry)
        return carry

    carry = lax.fori_loop(0, count, group, carry)
    for k in range(first + count * unroll, last):
        carry = body(k, carry)
    return carry


def tile(k):
    return pl.ds(pl.multiple_of(8 * (k + 1), 8), 8)


def density(temp, salt):
    return HALINE * salt - THERMAL * temp


def tile_update(k, fields, above, below, around, wet, wet_v, wet_around, press, press_around, cor, bat, base, half):
    signs = (-1.0, 1.0, -1.0, 1.0)
    speeds = (fields[2], fields[2], fields[3], fields[3])
    ways = [b + v * h if s > 0 else b - v * h for b, h, v, s in zip(base, half, speeds, signs)]
    own = SIDE * wet_v
    for way, wet_n in zip(ways, wet_around):
        own = own + way * wet_n
    tend = []
    for f, up, down, sides in zip(fields, above, below, around):
        t = SIDE * (up + down) - own * f
        for way, q in zip(ways, sides):
            t = t + way * q
        tend.append(t)
    slopes = [h * (m - press * w) for h, m, w in zip(half, press_around, wet_around)]
    rate = jnp.where(bat == lax.convert_element_type(k + 1, jnp.float32), DRAG, 0.0)
    tend[2] = tend[2] + (cor * fields[3] - (slopes[0] - slopes[1]) - rate * fields[2])
    tend[3] = tend[3] - (cor * fields[2] + (slopes[2] - slopes[3]) + rate * fields[3])
    scale = STEP * wet
    return [f + scale * t for f, t in zip(fields, tend)]


def from_side(centre, other, way, to_u, to_v):
    scale = STEP * centre[4]
    wet_n = other[4]
    adds = [scale * (way * (other[i] - wet_n * centre[i])) for i in range(4)]
    push = (0.5 * scale) * (wet_n * (other[5] - centre[5]))
    if to_u:
        adds[2] = adds[2] + to_u * push
    if to_v:
        adds[3] = adds[3] + to_v * push
    return adds


def way_of(cell, side):
    if side == "east":
        return SIDE - 0.5 * cell[2]
    if side == "west":
        return SIDE + 0.5 * cell[2]
    if side == "north":
        return SIDE - 0.5 * cell[3]
    return SIDE + 0.5 * cell[3]


PUSH = {"east": (-1.0, 0.0), "west": (1.0, 0.0), "north": (0.0, -1.0), "south": (0.0, 1.0)}


def side_adds(cell, other, side):
    return from_side(cell, other, way_of(cell, side), *PUSH[side])


def iotas(shape=(8, 128)):
    return lax.broadcasted_iota(jnp.int32, shape, 0), lax.broadcasted_iota(jnp.int32, shape, 1)


def swap(value):
    _, lane = iotas(value.shape)
    return jnp.where(lane % 2 == 0, pltpu.roll(value, 127, 1), pltpu.roll(value, 1, 1))


def level_of(lane, odd):
    return jnp.where(lane % 2 == odd, lane // 2, LOW + lane // 2)


def running(odd):
    row, col = iotas((128, 128))
    row, col = level_of(row, odd), level_of(col, odd)
    return jnp.where(row < col, 1.0, jnp.where(row == col, 0.5, 0.0))


def merged(west, east):
    _, lane = iotas()
    even = lane % 2 == 0
    return (
        [jnp.where(even, w, pltpu.roll(e, 126, 1)) for w, e in zip(west, east)],
        [jnp.where(even, e, w) for w, e in zip(west, east)],
    )


def turn_of(k, high):
    return (127 - 2 * (k - LOW)) if high else (128 - 2 * k)


def first_kernel(levels, place, temp_hbm, salt_hbm, east_hbm, north_hbm, sea_hbm, bat_hbm, cor_hbm,
                 part, wet_ref, on, off, state, planes, press, temp, salt, east, north, sea, bat_ref, sems, plane_sems):
    chunk = 25 if levels % 25 == 0 else levels
    chunks = levels // chunk
    inputs = ((temp_hbm, temp), (salt_hbm, salt), (east_hbm, east), (north_hbm, north), (sea_hbm, sea))

    def copy_of(i, c):
        source, target = inputs[i]
        rows = pl.ds(c * chunk, chunk)
        return pltpu.make_async_copy(source.at[rows], target.at[rows], sems.at[i, c])

    plane_copies = [
        pltpu.make_async_copy(bat_hbm, bat_ref, plane_sems.at[0]),
        pltpu.make_async_copy(cor_hbm, planes.at[1], plane_sems.at[1]),
    ]
    for copy in plane_copies:
        copy.start()
    for c in range(chunks):
        for i in range(5):
            copy_of(i, c).start()
    lon_odd = place[0] % 2
    sub, lane = iotas()
    zero = jnp.zeros((8, 128), jnp.float32)
    for i in range(4):
        for edge in (-1, levels):
            state[i, pl.ds(8 * (edge + 1), 8), :] = zero
            part[i, pl.ds(8 * (edge + 1), 8), :] = zero
    for edge in (-1, levels):
        wet_ref[pl.ds(8 * (edge + 1), 8), :] = zero
    for copy in plane_copies:
        copy.wait()
    depth = bat_ref[...]
    bat = depth.astype(jnp.float32)
    planes[0] = bat
    cor = planes[1]

    def prepare(k, total):
        wet = jnp.where(k < depth, sea[k], 0).astype(jnp.float32)
        fields = [ref[k] * wet for ref in (temp, salt, east, north)]
        for i in range(4):
            state[i, tile(k), :] = fields[i]
        wet_ref[tile(k), :] = wet
        dens = density(fields[0], fields[1])
        total = total + dens
        press[tile(k), :] = GRAVITY * (total - 0.5 * dens)
        return total

    total = zero
    for c in range(chunks):
        for i in range(5):
            copy_of(i, c).wait()
        total = levels_loop(c * chunk, (c + 1) * chunk, UNROLL_A, prepare, total)

    open_sides = [ok.astype(jnp.float32) for ok in (lane < 127, lane > 0, sub < 7, sub > 0)]
    base = [SIDE * ok for ok in open_sides]
    half = [0.5 * ok for ok in open_sides]

    def beside(value):
        return (pltpu.roll(value, 127, 1), pltpu.roll(value, 1, 1), pltpu.roll(value, 7, 0), pltpu.roll(value, 1, 0))

    def partial(k, carry):
        fields = [state[i, tile(k), :] for i in range(4)]
        above = [state[i, tile(k - 1), :] for i in range(4)]
        below = [state[i, tile(k + 1), :] for i in range(4)]
        wet = wet_ref[tile(k), :]
        wet_v = wet_ref[tile(k - 1), :] + wet_ref[tile(k + 1), :]
        p = press[tile(k), :]
        new = tile_update(k, fields, above, below, [beside(f) for f in fields], wet, wet_v, beside(wet),
                          p, beside(wet * p), cor, bat, base, half)
        for i in range(4):
            part[i, tile(k), :] = new[i]
        return carry

    levels_loop(0, levels, UNROLL_B, partial, 0)

    pair = lane // 2
    packed = {}
    for first, last in ((0, min(LOW, levels)), (LOW, levels)):
        columns = [zero] * 10
        for k in range(first, last):
            here = pair == k - first
            at = pl.ds(8 * (k + 1), 8)
            values = [state[i, at, :] for i in range(4)] + [wet_ref[at, :], press[at, :]]
            values = values + [part[i, at, :] for i in range(4)]
            columns = [jnp.where(here, pltpu.roll(v, 2 * (k - first) + 1, 1), c) for v, c in zip(values, columns)]
        packed[first] = columns
    even = lane % 2 == 0
    for j, (low, high) in enumerate(zip(packed[0], packed[LOW])):
        eastern = jnp.where(even, low, pltpu.roll(high, 1, 1))
        west = jnp.where(even, pltpu.roll(high, 127, 1), low)
        on[j] = jnp.where(lon_odd == 0, eastern, west)
        off[j] = jnp.where(lon_odd == 0, west, eastern)


def write_rows(levels, ref, row, state, wet_ref, part):
    rows = pl.ds(8 + row, levels, stride=8)
    planes = [state[i, rows, :] for i in range(4)] + [wet_ref[rows, :]] + [part[i, rows, :] for i in range(4)]
    for i, plane in enumerate(planes):
        ref[pl.ds(levels * i, levels), :] = plane
    left = long_of(levels) - 9 * levels
    if left:
        ref[pl.ds(9 * levels, left), :] = jnp.zeros((left, 128), jnp.float32)


def long_of(levels):
    return 8 * ((9 * levels + 7) // 8)


def rows_kernel(levels, tops, place, state, wet_ref, part, xs, fold_a):
    lat_odd = place[1] % 2
    write_rows(levels, xs, 7 - 7 * lat_odd, state, wet_ref, part)

    @pl.when(place[1] == tops)
    def _():
        rows = pl.ds(8 + 7, levels, stride=8)
        planes = [state[i, rows, :] for i in range(4)] + [wet_ref[rows, :]] + [part[i, rows, :] for i in range(4)]
        for i, plane in enumerate(planes):
            count = min(levels, PART - levels * i)
            if count > 0:
                fold_a[pl.ds(levels * i, count), :] = plane[:count]


def sides_of(lon_odd, on_own, off_own, on, off):
    odd = lon_odd == 1
    west = [swap(jnp.where(odd, on_own[j], off_own[j])) for j in range(10)]
    east = [swap(jnp.where(odd, off_own[j], on_own[j])) for j in range(10)]
    far_west = [jnp.where(odd, on[j], off[j]) for j in range(10)]
    far_east = [jnp.where(odd, off[j], on[j]) for j in range(10)]
    return west, east, far_west, far_east


def corner_kernel(levels, tops, place, on_own, off_own, on, off, state, wet_ref, part, xs_own, zb, fold_b, corner_xs, extra):
    lon_odd = place[0] % 2
    lat_odd = place[1] % 2
    write_rows(levels, zb, 7 * lat_odd, state, wet_ref, part)
    west, east, far_west, far_east = sides_of(lon_odd, on_own, off_own, on, off)
    adds_w = side_adds(west[:6], far_west[:6], "west")
    adds_e = side_adds(east[:6], far_east[:6], "east")
    entries = far_west[:6] + adds_w + far_east[:6] + adds_e
    for ref, start, flag in ((corner_xs, 0, lat_odd == 0), (zb, long_of(levels), lat_odd == 1)):
        for r, entry in enumerate(entries):
            ref[pl.ds(start + r, 1), :] = jnp.where(flag, entry[7:8, :], entry[0:1, :])
        ref[pl.ds(start + 20, 4), :] = jnp.zeros((4, 128), jnp.float32)
    low, high = merged(adds_w, adds_e)
    for i in range(4):
        extra[i] = low[i]
        extra[4 + i] = high[i]

    @pl.when(place[1] == tops)
    def _():
        fold_b[...] = zb[pl.ds(PART, zb.shape[0] - PART), :]


def second_kernel(levels, place, part, extra, full):
    _, lane = iotas()
    ends = (lane == 0) | (lane == 127)

    def add(extra, high, k, carry):
        for i in range(4):
            more = jnp.where(ends, pltpu.roll(extra[i], turn_of(k, high), 1), 0.0)
            full[i, tile(k), :] = part[i, tile(k), :] + more
        return carry

    levels_loop(0, min(LOW, levels), UNROLL_C, functools.partial(add, [extra[i] for i in range(4)], False), 0)
    if levels > LOW:
        levels_loop(LOW, levels, UNROLL_C, functools.partial(add, [extra[4 + i] for i in range(4)], True), 0)
    zero = jnp.zeros((8, 128), jnp.float32)
    for i in range(4):
        for edge in (-1, levels):
            full[i, pl.ds(8 * (edge + 1), 8), :] = zero


def choose_kernel(levels, count, place, zb, corner_xs, *refs):
    corners = refs[count]
    odd = place[1] % 2 == 1
    at_end = pl.ds(long_of(levels), 24)
    corners[pl.ds(0, 24), :] = jnp.where(odd, corner_xs[...], zb[at_end, :])
    corners[pl.ds(24, 24), :] = jnp.where(odd, zb[at_end, :], corner_xs[...])


def third_kernel(levels, tops, place, full_in, wet_ref, columns_in, xs_own, zb_own, xs, zb, fold_a, fold_b,
                 on_own, off_own, on, off, corners,
                 temp_hbm, salt_hbm, east_hbm, north_hbm, full, halo, flipped, turned, outs, sems):
    lon_odd = place[0] % 2
    lat_odd = place[1] % 2
    odd = lat_odd == 1
    top = place[1] == tops
    sub, lane = iotas()
    bat, cor = columns_in[0], columns_in[1]
    full[...] = full_in[...]

    south_c = corners[pl.ds(0, 24), :]
    north_c = jnp.where(top, fold_b[pl.ds(long_of(levels) - PART, 24), :], corners[pl.ds(24, 24), :])
    r = lax.broadcasted_iota(jnp.int32, (24, 128), 0)
    swapped = swap(jnp.concatenate([north_c[10:20], north_c[0:10], north_c[20:24]], axis=0))
    s = r % 10
    swapped = jnp.where((s == 2) | (s == 3) | (s == 8) | (s == 9), -swapped, swapped)
    north_c = jnp.where(top, swapped, north_c)

    west, east, far_west, far_east = sides_of(lon_odd, on_own, off_own, on, off)
    far_cols = []
    for own, far, toward, base, order in ((west, far_west, "east", 0, 0), (east, far_east, "west", 10, 1)):
        new = list(far[6:10])
        south_cell = [south_c[base + i : base + i + 1, :] for i in range(6)]
        north_cell = [north_c[base + i : base + i + 1, :] for i in range(6)]
        for i, a in enumerate(side_adds(far[:6], own[:6], toward)):
            new[i] = new[i] + a
        for i, a in enumerate(side_adds(far[:6], south_cell, "south")):
            new[i] = new[i] + jnp.where(sub == 0, a, 0.0)
        for i, a in enumerate(side_adds(far[:6], north_cell, "north")):
            new[i] = new[i] + jnp.where(sub == 7, a, 0.0)
        p = GRAVITY * jnp.dot(density(new[0], new[1]), running(order), precision=HIGH,
                              preferred_element_type=jnp.float32)
        far_cols.append(new + [far[4] * p, far[4]])

    @pl.when(jnp.logical_not(top))
    def _():
        flipped[...] = jnp.where(odd, zb[pl.ds(0, long_of(levels)), :], xs[...])

    @pl.when(top)
    def _():
        mirror = 127 - lane
        for t in range(flipped.shape[0] // 8):
            at = 8 * t
            rows = fold_a[pl.ds(at, 8), :] if at < PART else fold_b[pl.ds(at - PART, 8), :]
            flipped[pl.ds(at, 8), :] = jnp.take_along_axis(rows, mirror, axis=1, mode="promise_in_bounds")

    def plane(ref, i):
        return ref[pl.ds(levels * i, levels), :]

    sign = jnp.where(top, -1.0, 1.0)
    signs = [1.0, 1.0, sign, sign, 1.0, 1.0, 1.0, sign, sign]
    north_far = [plane(flipped, i) * signs[i] for i in range(9)]
    south_far = [jnp.where(odd, plane(xs, i), plane(zb, i)) for i in range(9)]
    north_own = [jnp.where(odd, plane(zb_own, i), plane(xs_own, i)) for i in range(5)]
    south_own = [jnp.where(odd, plane(xs_own, i), plane(zb_own, i)) for i in range(5)]
    row, col = iotas((levels, levels))
    lower = jnp.where(col < row, 1.0, jnp.where(row == col, 0.5, 0.0))

    def pressures(planes):
        dens = jnp.concatenate([density(f[0], f[1]) for f in planes], axis=1)
        p = GRAVITY * jnp.dot(lower, dens, precision=HIGH, preferred_element_type=jnp.float32)
        return [p[:, 128 * j : 128 * j + 128] for j in range(len(planes))]

    before = pressures([south_far, north_far, south_own, north_own])
    lanes = lax.broadcasted_iota(jnp.int32, (levels, 128), 1)
    turned[...] = jnp.concatenate([south_c, north_c, jnp.zeros((80, 128), jnp.float32)], axis=0).T

    def in_order(odd_first):
        low = min(LOW, levels)
        parts = [turned[pl.ds(odd_first, low, stride=2), :]]
        if levels > LOW:
            parts.append(turned[pl.ds(1 - odd_first, levels - LOW, stride=2), :])
        return jnp.concatenate(parts, axis=0)

    west_c, east_c = in_order(0), in_order(1)
    results = []
    for n, (far, own, own_side, far_side, own_row) in enumerate(
        ((south_far, south_own, "south", "north", 0), (north_far, north_own, "north", "south", 7))
    ):
        far_cell = far[:5] + [before[n]]
        own_cell = own[:5] + [before[2 + n]]
        rows = pl.ds(8 + own_row, levels, stride=8)
        for i, a in enumerate(side_adds(own_cell, far_cell, own_side)):
            full[i, rows, :] = full[i, rows, :] + a
        new = []
        for i, a in enumerate(side_adds(far_cell, own_cell, far_side)):
            c = 24 * n + 6 + i
            extra = jnp.where(lanes == 0, west_c[:, c : c + 1], 0.0)
            extra = jnp.where(lanes == 127, east_c[:, c + 10 : c + 11], extra)
            new.append(far[5 + i] + a + extra)
        results.append(new)
    later = pressures(results)
    for n, (new, far) in enumerate(zip(results, (south_far, north_far))):
        for i, value in enumerate(new + [far[4] * later[n], far[4]]):
            halo[n, i, pl.ds(0, levels), :] = value

    chunk = 25 if levels % 25 == 0 else levels

    def copy_of(i, c):
        rows = pl.ds(c * chunk, chunk)
        target = (temp_hbm, salt_hbm, east_hbm, north_hbm)[i]
        return pltpu.make_async_copy(outs.at[i, rows], target.at[rows], sems.at[i, c])

    def beside(value, k, j, extra, high):
        far = pltpu.roll(extra[j], turn_of(k, high), 1)
        return (
            jnp.where(lane == 127, far, pltpu.roll(value, 127, 1)),
            jnp.where(lane == 0, far, pltpu.roll(value, 1, 1)),
            jnp.where(sub == 7, halo[1, j, pl.ds(k, 1), :], pltpu.roll(value, 7, 0)),
            jnp.where(sub == 0, halo[0, j, pl.ds(k, 1), :], pltpu.roll(value, 1, 0)),
        )

    base = [SIDE] * 4
    half = [0.5] * 4

    def last_step(extra, high, k, total):
        fields = [full[i, tile(k), :] for i in range(4)]
        above = [full[i, tile(k - 1), :] for i in range(4)]
        below = [full[i, tile(k + 1), :] for i in range(4)]
        wet = wet_ref[tile(k), :]
        wet_v = wet_ref[tile(k - 1), :] + wet_ref[tile(k + 1), :]
        dens = density(fields[0], fields[1])
        total = total + dens
        p = GRAVITY * (total - 0.5 * dens)
        new = tile_update(k, fields, above, below, [beside(f, k, i, extra, high) for i, f in enumerate(fields)],
                          wet, wet_v, beside(wet, k, 5, extra, high), p, beside(wet * p, k, 4, extra, high),
                          cor, bat, base, half)
        for i in range(4):
            outs[i, k] = new[i]
        return total

    extras = merged(far_cols[0], far_cols[1])
    total = jnp.zeros((8, 128), jnp.float32)
    for c in range(levels // chunk):
        first, last = c * chunk, (c + 1) * chunk
        for start, stop, high in ((first, min(last, LOW), False), (max(first, LOW), last, True)):
            if start < stop:
                total = levels_loop(start, stop, UNROLL_D, functools.partial(last_step, extras[int(high)], high), total)
        for i in range(4):
            copy_of(i, c).start()
    for c in range(levels // chunk):
        for i in range(4):
            copy_of(i, c).wait()


def shape(*dims):
    return jax.ShapeDtypeStruct(dims, jnp.float32)


def call(kernel, outs, ins, scratch=(), far_ins=(), far_outs=False, work=2*10**10):
    vmem = pl.BlockSpec(memory_space=pltpu.VMEM)
    hbm = pl.BlockSpec(memory_space=pltpu.HBM)
    anywhere = pl.BlockSpec(memory_space=pl.ANY)
    return pl.pallas_call(
        kernel,
        out_shape=outs,
        in_specs=[pl.BlockSpec(memory_space=pltpu.SMEM)] + [anywhere if i in far_ins else vmem for i in range(1, len(ins))],
        out_specs=[hbm if far_outs else vmem] * len(outs),
        scratch_shapes=list(scratch),
        compiler_params=pltpu.CompilerParams(vmem_limit_bytes=20 * 2**20),
        cost_estimate=pl.CostEstimate(flops=work, bytes_accessed=1000, transcendentals=0),
    )(*ins)


def pairs_of(names, count_lon, count_lat):
    def at(lon, lat):
        return lon * count_lat + lat if names[0] == "lon" else lat * count_lon + lon

    every = [(lon, lat) for lon in range(count_lon) for lat in range(count_lat)]
    on = [(at(o, a), at(o ^ 1, a)) for o, a in every]
    off = [(at(o, a), at((o + 1 if o % 2 else o - 1) % count_lon, a)) for o, a in every]
    xs = [(at(o, a), at(o, a ^ 1)) for o, a in every]
    zb = [(at(o, a), at(o, a + 1 if a % 2 else a - 1)) for o, a in every if 0 < a < count_lat - 1]
    top = count_lat - 1
    to_relay = [(at(o, top), at(o ^ 3, top - 1)) for o in range(count_lon)]
    from_relay = [(at(o ^ 3, top - 1), at(count_lon - 1 - o, top)) for o in range(count_lon)]
    return on, off, xs, zb, to_relay, from_relay


def per_device(names, count_lon, count_lat, temp, salt, east, north, sea, bathymetry, vorticity):
    levels = temp.shape[0]
    on_pairs, off_pairs, xs_pairs, zb_pairs, to_relay, from_relay = pairs_of(names, count_lon, count_lat)
    place = jnp.stack([lax.axis_index("lon"), lax.axis_index("lat")]).astype(jnp.int32)
    tall = 8 * (levels + 2)
    ten = shape(10, 8, 128)
    long = long_of(levels)
    message = shape(long, 128)
    cube = (levels, 8, 128)
    chunks = 3 if levels % 25 == 0 else 1
    raw = [pltpu.with_memory_space_constraint(x, pltpu.HBM) for x in (temp, salt, east, north, sea, bathymetry, vorticity)]
    part, wet, on_own, off_own, state, columns = call(
        functools.partial(first_kernel, levels),
        [shape(4, tall, 128), shape(tall, 128), ten, ten, shape(4, tall, 128), shape(2, 8, 128)],
        [place, *raw],
        [pltpu.VMEM((tall, 128), jnp.float32)] + [pltpu.VMEM(cube, jnp.float32)] * 4
        + [pltpu.VMEM(cube, jnp.int32), pltpu.VMEM((8, 128), jnp.int32), pltpu.SemaphoreType.DMA((5, chunks)),
           pltpu.SemaphoreType.DMA((2,))],
        far_ins=(1, 2, 3, 4, 5, 6, 7),
    )
    move = functools.partial(lax.ppermute, axis_name=names)
    on = move(on_own, perm=on_pairs)
    off = move(off_own, perm=off_pairs)
    xs_own, fold_a = call(
        functools.partial(rows_kernel, levels, count_lat - 1),
        [message, shape(PART, 128)],
        [place, state, wet, part],
        work=W_ROWS,
    )
    fold_a = move(fold_a, perm=to_relay)
    xs = move(xs_own, perm=xs_pairs)
    zb_own, fold_b, corner_xs, extra = call(
        functools.partial(corner_kernel, levels, count_lat - 1),
        [shape(long + 24, 128), shape(long + 24 - PART, 128), shape(24, 128), shape(8, 8, 128)],
        [place, on_own, off_own, on, off, state, wet, part, xs_own],
        work=W_CORNER,
    )
    fold_b = move(fold_b, perm=to_relay)
    zb = move(zb_own, perm=zb_pairs)
    corner_xs = move(corner_xs, perm=xs_pairs)
    fold_a = move(fold_a, perm=from_relay)
    fold_b = move(fold_b, perm=from_relay)
    full, = call(functools.partial(second_kernel, levels), [shape(4, tall, 128)], [place, part, extra], work=W_ADD)
    corners, = call(
        functools.partial(choose_kernel, levels, 2),
        [shape(48, 128)],
        [place, zb, corner_xs, xs, fold_a],
        far_ins=(3, 4),
        work=W_CHOOSE,
    )
    out = shape(levels, 8, 128)
    return tuple(
        call(
            functools.partial(third_kernel, levels, count_lat - 1),
            [out] * 4,
            [place, full, wet, columns, xs_own, zb_own, xs, zb, fold_a, fold_b, on_own, off_own, on, off,
             corners],
            [
                pltpu.VMEM((4, tall, 128), jnp.float32),
                pltpu.VMEM((2, 6, 8 * ((levels + 7) // 8), 128), jnp.float32),
                pltpu.VMEM((long, 128), jnp.float32),
                pltpu.VMEM((128, 128), jnp.float32),
                pltpu.VMEM((4,) + cube, jnp.float32),
                pltpu.SemaphoreType.DMA((4, chunks)),
            ],
            far_outs=True,
        )
    )


def solution(mesh):
    cube, plane = P(None, "lat", "lon"), P("lat", "lon")
    names = tuple(n for n in mesh.axis_names if n in ("lon", "lat"))
    return jax.shard_map(
        functools.partial(per_device, names, mesh.shape["lon"], mesh.shape["lat"]),
        mesh=mesh,
        in_specs=(cube,) * 5 + (plane,) * 2,
        out_specs=(cube,) * 4,
        check_vma=False,
    )
```
